256 devices in a mesh: dp: 32 (over z_lo, y, x), ctx: 8 (over z_hi, core).
Axes of the slice: x: 4, y: 4, z: 8 (z_hi: 4, z_lo: 2; z = z_hi * 2 + z_lo), core: 2. Of those that a mesh axis runs over, the one named last changes fastest.
Arguments:
- inputs: bfloat16 [32768, 1024], P(('dp', 'ctx')), may hold values from -6 to 6
- input_weight: bfloat16 [1024, 4096], P('dp'), may hold values from -0.1875 to 0.1875
- output_weight: bfloat16 [1024, 1024], P('dp'), may hold values from -0.1875 to 0.1875
- cotangent: bfloat16 [32768, 1024], P(('dp', 'ctx')), may hold values from -6 to 6
- lengths: int32 [32, 4], P('dp'), may hold values from 1 to 768, 1024 in all within a row
- buckets: int32 [1024], replicated, may hold values from 0 to 31
- bias_weights: float32 [8, 32], replicated, may hold values from -4 to 4
Outputs:
- outputs: bfloat16 [32768, 1024], P(('dp', 'ctx'))
- input_grads: bfloat16 [32768, 1024], P(('dp', 'ctx'))
- weight_grads: float32 [1024, 1024], P('dp', 'ctx')
The draws below stay inside these ranges and needn't reach their ends.
Inputs may be any that keep to these rules, and one draw needn't show every extreme that they name: Each row holds the 4 history lengths of one group, summing to 1024; the longest is exactly 768.
All inputs are finite; a program needn't handle non-finite values.
Results may differ from the reference program's by a relative error of at most 0.034.
Values may be sent and summed in bfloat16 or wider, within the bound.
A program may use at most 256 MiB of HBM per device.

```python
import math
import jax
import jax.numpy as jnp
import numpy as np
from jax import lax

D = 1024
H = 8
NB = 32
USERS = 4
ROWS = 128
SEQ = 1024
MOST = 768
GROUPS = 32
TOKENS = 32768


def place_ends(drawn, key, smallest, high):
    index_at = [jax.random.randint(jax.random.fold_in(key, axis), (), 0, length) for axis, length in enumerate(drawn.shape)]
    widest = drawn.shape.index(max(drawn.shape))
    next_to = index_at[:widest] + [(index_at[widest] + 1) % drawn.shape[widest]] + index_at[widest + 1:]
    return drawn.at[tuple(index_at)].set(smallest).at[tuple(next_to)].set(high)


def block_scale(rng, extent, shards, low, high):
    gain = 1.0
    for position, blocks in shards:
        draws = jax.random.uniform(jax.random.fold_in(jax.random.fold_in(rng, 6), position), (blocks,), jnp.float32, low / len(shards), high / len(shards))
        gain = gain * jnp.repeat(jnp.exp(draws), extent[position] // blocks).reshape((-1,) + (1,) * (len(extent) - 1 - position))
    return gain


def profile(amount, total, limit, slope):
    portions = [(1 << 20) // math.isqrt(grade ** slope) + 1 for grade in range(2, amount + 1)]
    spare, counts = total - limit - (amount - 1), [1] * (amount - 1)
    while spare > 0:
        candidates = [i for i in range(amount - 1) if counts[i] < limit]
        whole, budget = sum([portions[i] for i in candidates]), spare
        for i in candidates:
            extra = min(limit - counts[i], max(1, budget * portions[i] // whole), spare)
            counts[i] = counts[i] + extra
            spare = spare - extra
    return np.array([limit] + counts)


def ragged(rng, number_of, total, bound, slope):
    if number_of == 2:
        one = jax.random.randint(rng, (), max(1, total - bound), min(bound, total - 1) + 1)
        return jnp.stack([one, total - one])
    tallies = jnp.asarray(profile(number_of, total, bound, slope), jnp.int32)
    pairs = (number_of - 1) // 2
    source_of, sink = tallies[1:1 + 2 * pairs:2], tallies[2:2 + 2 * pairs:2]
    margin = jnp.minimum(source_of - 1, bound - sink)
    passed = jax.random.randint(jax.random.fold_in(rng, 1), (pairs,), 0, 1 << 20) % (margin + 1)
    tallies = tallies.at[1:1 + 2 * pairs:2].set(source_of - passed).at[2:2 + 2 * pairs:2].set(sink + passed)
    return tallies[jax.random.permutation(jax.random.fold_in(rng, 2), number_of)]


def normal_values(stream_key, extent, spread, bound, shards=(), held_as=jnp.bfloat16):
    drawn = spread * jax.random.normal(stream_key, extent, jnp.float32)
    if shards:
        drawn = drawn * block_scale(stream_key, extent, shards, -0.22, 0.18)
    return jnp.clip(drawn, -bound, bound).astype(held_as)


def setup_inputs(seed: int = 0) -> dict:
    streams_of = jax.random.split(jax.random.key(seed), 8)
    inputs = normal_values(streams_of[0], (TOKENS, D), 1.0, 6.0, ((0, 256),))
    input_weight = normal_values(streams_of[1], (D, 4 * D), D ** -0.5, 0.1875, ((0, 32),))
    output_weight = normal_values(streams_of[2], (D, D), D ** -0.5, 0.1875, ((0, 32),))
    cotangent = normal_values(streams_of[3], (TOKENS, D), 1.0, 6.0, ((0, 256),))
    lengths = jax.vmap(lambda own: ragged(own, USERS, SEQ, MOST, 2))(jax.random.split(streams_of[4], GROUPS)).reshape((GROUPS, USERS)).astype(jnp.int32)
    buckets = place_ends(jax.random.randint(streams_of[5], (SEQ,), 0, NB), jax.random.fold_in(streams_of[5], 1), 0, NB - 1).astype(jnp.int32)
    bias_weights = normal_values(streams_of[6], (H, NB), 1.0, 4.0, (), jnp.float32)
    return {"inputs": inputs, "input_weight": input_weight, "output_weight": output_weight, "cotangent": cotangent, "lengths": lengths, "buckets": buckets, "bias_weights": bias_weights}


EPSILON = 1e-06

def rounded(values):
    return lax.optimization_barrier(values.astype(jnp.bfloat16)).astype(jnp.float32)

def silu_grad(values):
    sigmoid = jax.nn.sigmoid(values)
    return sigmoid * (1.0 + values * (1.0 - sigmoid))

def normalize(values):
    average = lax.optimization_barrier(jnp.mean(values, axis=-1, keepdims=True))
    centered = values - average
    inverse = lax.rsqrt(lax.optimization_barrier(jnp.mean(centered * centered, axis=-1, keepdims=True)) + EPSILON)
    return (centered * inverse, inverse)

def normalize_back(normed, inverse, upstream):
    first = lax.optimization_barrier(jnp.mean(upstream, axis=-1, keepdims=True))
    second = lax.optimization_barrier(jnp.mean(upstream * normed, axis=-1, keepdims=True))
    return (upstream - first - normed * second) * inverse

def group_pass(inputs_group, grads_group, lengths_row, input_weight, output_weight, bias_table):
    seq = inputs_group.shape[0]
    width = output_weight.shape[0]
    heads = bias_table.shape[0]
    head_size = width // heads
    scale = 1.0 / math.sqrt(head_size)
    positions = jnp.arange(seq, dtype=jnp.int32)
    boundary = jnp.cumsum(lengths_row).astype(jnp.int32)
    segments = lax.optimization_barrier(jnp.sum((positions[:, None] >= boundary[None, :]).astype(jnp.int32), axis=1))
    allowed = (segments[:, None] == segments[None, :]) & (positions[None, :] <= positions[:, None])
    distance = jnp.maximum(positions[:, None] - positions[None, :], 0)
    bias = jnp.take(bias_table, distance, axis=1)
    normed_x, inverse_x = normalize(inputs_group.astype(jnp.float32))
    pre = jnp.dot(normed_x.astype(jnp.bfloat16), input_weight, preferred_element_type=jnp.float32)
    acts = rounded(jax.nn.silu(pre))
    update_gate = acts[:, :width]
    values = acts[:, width:2 * width].reshape(seq, heads, head_size)
    queries = acts[:, 2 * width:3 * width].reshape(seq, heads, head_size)
    key_rows = acts[:, 3 * width:].reshape(seq, heads, head_size)
    scores = jnp.einsum('shd,thd->hst', queries, key_rows) * scale + bias
    weights = rounded(jnp.where(allowed[None], jax.nn.silu(scores) / seq, 0.0))
    attended = jnp.einsum('hst,thd->shd', weights, values).reshape(seq, width)
    normed_o, inverse_o = normalize(attended)
    gated = (normed_o * update_gate).astype(jnp.bfloat16)
    outputs = (inputs_group.astype(jnp.float32) + jnp.dot(gated, output_weight, preferred_element_type=jnp.float32)).astype(jnp.bfloat16)
    weight_term = jnp.dot(gated.T, grads_group, preferred_element_type=jnp.float32)
    d_gated = jnp.dot(grads_group, output_weight.T, preferred_element_type=jnp.float32)
    d_update = d_gated * normed_o
    d_attended = rounded(normalize_back(normed_o, inverse_o, d_gated * update_gate))
    grad_heads = d_attended.reshape(seq, heads, head_size)
    d_weights = jnp.einsum('shd,thd->hst', grad_heads, values)
    d_scores = rounded(jnp.where(allowed[None], d_weights * silu_grad(scores) / seq, 0.0))
    d_queries = jnp.einsum('hst,thd->shd', d_scores, key_rows) * scale
    blocks = seq // ROWS
    score_blocks = d_scores.reshape(heads, blocks, ROWS, seq)
    weight_blocks = weights.reshape(heads, blocks, ROWS, seq)
    query_blocks = queries.reshape(blocks, ROWS, heads, head_size)
    grad_blocks = grad_heads.reshape(blocks, ROWS, heads, head_size)
    d_keys = lax.optimization_barrier(jnp.sum(rounded(jnp.einsum('hbst,bshd->bthd', score_blocks, query_blocks) * scale), axis=0))
    d_values = lax.optimization_barrier(jnp.sum(rounded(jnp.einsum('hbst,bshd->bthd', weight_blocks, grad_blocks)), axis=0))
    d_acts = jnp.concatenate([d_update, d_values.reshape(seq, width), d_queries.reshape(seq, width), d_keys.reshape(seq, width)], axis=1)
    d_pre = (d_acts * silu_grad(pre)).astype(jnp.bfloat16)
    d_normed = jnp.dot(d_pre, input_weight.T, preferred_element_type=jnp.float32)
    input_grads = (grads_group.astype(jnp.float32) + normalize_back(normed_x, inverse_x, d_normed)).astype(jnp.bfloat16)
    return (outputs, input_grads, weight_term)

def reference(inputs, input_weight, output_weight, cotangent, lengths, buckets, bias_weights):
    bias_table = bias_weights[:, buckets]
    groups = lengths.shape[0]
    width = inputs.shape[1]
    seq = inputs.shape[0] // groups

    def one_group(items):
        inputs_group, grads_group, lengths_row = items
        return group_pass(inputs_group, grads_group, lengths_row, input_weight, output_weight, bias_table)
    outputs, input_grads, terms = lax.map(one_group, (inputs.reshape(groups, seq, width), cotangent.reshape(groups, seq, width), lengths))
    return (outputs.reshape(groups * seq, width), input_grads.reshape(groups * seq, width), lax.optimization_barrier(jnp.sum(terms, axis=0)))
```

```python
import functools
import math

import jax
import jax.numpy as jnp
from jax import lax
from jax.experimental import pallas as pl
from jax.experimental.pallas import tpu as pltpu
from jax.sharding import PartitionSpec as P

EPSILON = 1e-06
MESH = pl.DeviceIdType.MESH
F32 = jnp.float32
BF16 = jnp.bfloat16

ROWS = 128
BLK = 256
NBLK = 4
HEADS = 8
HD = 128
D = 1024
SEQ = 1024
PLANE = 16
PAIRS = NBLK * (NBLK + 1) // 2
SCALE = 1.0 / math.sqrt(HD)


def nn(a, b):
    return lax.dot_general(a, b, (((1,), (0,)), ((), ())), preferred_element_type=F32)


def nt(a, b):
    return lax.dot_general(a, b, (((1,), (1,)), ((), ())), preferred_element_type=F32)


def tn(a, b):
    return lax.dot_general(a, b, (((0,), (0,)), ((), ())), preferred_element_type=F32)


def sigmoid(values):
    return 0.5 * jnp.tanh(0.5 * values) + 0.5


def normalize(values):
    average = jnp.mean(values, axis=-1, keepdims=True)
    centered = values - average
    inverse = lax.rsqrt(jnp.mean(centered * centered, axis=-1, keepdims=True) + EPSILON)
    return (centered * inverse, inverse)


def kernel(
    lengths_ref, bias_ref, buckets_ref, x_ref, win_ref, wout_ref, ct_ref,
    out_ref, grads_ref, wg_ref,
    xg, wa, wb, wra, wrb, wct, pret, actt, krow, vrow, wts, sgs, toep, attt, uf,
    dgs, dgr, stat, statr, gts, gtr, dat, dqt, dkt, dvt, dpt,
    wgd, wgdr, wgs, wgr, wzs, wzr,
    pd, pdr, ps, pr, own,
    xs, xr, xfs, xfr, was, war, wps, wpr, wos, wor, dss, dsr, sts, strr, gss, gsr,
    wds, wdr, wgss, wgsr, wzss, wzsr, pds, pdsr, pss, psr,
):
    dp = lax.axis_index("dp")
    ctx = lax.axis_index("ctx")
    zh, core = ctx // 2, ctx % 2
    zl, yx = dp // PLANE, dp % PLANE
    y, x = yx // 4, yx % 4
    mate = (dp, zh * 2 + 1 - core)

    def ctx_peer(t):
        return (ctx + t) % 8

    def plane_peer(t):
        return ((y + t // 4) % 4) * 4 + (x + t % 4) % 4

    def plane_from(t):
        return ((y + 4 - t // 4) % 4) * 4 + (x + 4 - t % 4) % 4

    def copy(src, dst, ss, rs, dev):
        return pltpu.make_async_remote_copy(
            src_ref=src, dst_ref=dst, send_sem=ss, recv_sem=rs, device_id=dev, device_id_type=MESH
        )

    barrier = pltpu.get_barrier_semaphore()

    def greet_ctx(t, _):
        pl.semaphore_signal(barrier, inc=1, device_id=(dp, ctx_peer(t)), device_id_type=MESH)
        return 0

    def greet_plane(t, _):
        pl.semaphore_signal(
            barrier, inc=1, device_id=(zl * PLANE + plane_peer(t), ctx), device_id_type=MESH
        )
        return 0

    def greet_column(t, _):
        pl.semaphore_signal(
            barrier, inc=1, device_id=((1 - zl) * PLANE + yx, t * 2 + core), device_id_type=MESH
        )
        return 0

    lax.fori_loop(1, 8, greet_ctx, 0)
    lax.fori_loop(1, 16, greet_plane, 0)
    lax.fori_loop(0, 4, greet_column, 0)

    normed, _ = normalize(x_ref[...].astype(F32))
    xg[ctx] = normed.astype(BF16)
    for part in range(4):
        at = pl.multiple_of(part * D + ctx * HD, HD)
        wa[zl, :, part * HD:(part + 1) * HD] = win_ref[:, pl.ds(at, HD)]
    wb[zl] = wout_ref[:, pl.ds(pl.multiple_of(core * 512, 512), 512)]

    pl.semaphore_wait(barrier, 26)

    other = ((1 - zl) * PLANE + yx, ctx)
    send_wa = copy(wa.at[zl], wa.at[zl], was.at[0], war.at[0], other)
    send_wa.start()
    send_x = [copy(xg.at[ctx], xg.at[ctx], xs.at[0], xr.at[0], mate)]
    for s in (2, 1, 3):
        send_x.append(
            copy(xg.at[ctx], xg.at[ctx], xs.at[s], xr.at[s], (dp, ((zh + s) % 4) * 2 + core))
        )
    for c in send_x:
        c.start()
    send_wb = copy(wb.at[zl], wb.at[zl], was.at[1], war.at[1], other)
    send_wb.start()

    def plane_send(src, dst, base):
        def step(t, _):
            copy(
                src, dst.at[:, yx], wps.at[base + t], wpr.at[base + t],
                (zl * PLANE + plane_peer(t), ctx),
            ).start()
            return 0
        lax.fori_loop(1, 16, step, 0)

    def plane_recv(src, dst, base):
        def step(t, _):
            copy(
                src, dst.at[:, plane_from(t)], wps.at[base + t], wpr.at[base + t],
                (zl * PLANE + plane_peer(t), ctx),
            ).wait_recv()
            return 0
        lax.fori_loop(1, 16, step, 0)

    def plane_done(src, dst, base):
        def step(t, _):
            copy(
                src, dst.at[:, yx], wps.at[base + t], wpr.at[base + t],
                (zl * PLANE + plane_peer(t), ctx),
            ).wait_send()
            return 0
        lax.fori_loop(1, 16, step, 0)

    send_wa.wait_recv()
    plane_send(wa, wra, 0)
    wra[:, yx] = wa[...]

    buckets = buckets_ref[...]
    table = jnp.zeros((1, SEQ), F32)
    for b in range(32):
        table = jnp.where(buckets == b, bias_ref[ctx, b], table)
    padded = jnp.concatenate([table[:, 0:BLK], table], axis=1)
    for d in range(NBLK):
        wide = jnp.broadcast_to(padded[:, d * BLK:d * BLK + 2 * BLK], (BLK, 2 * BLK))
        toep[d] = pltpu.roll(wide, 0, 1, stride=1, stride_axis=0)[:, BLK:]

    send_wb.wait_recv()
    wrb[core, :, yx] = wb[...]
    plane_recv(wa, wra, 0)
    plane_send(wb, wrb.at[core], 16)

    for part in range(4):
        piece = wra[:, :, :, part * HD:(part + 1) * HD].reshape(D, HD)
        wct[part * HD:(part + 1) * HD, :] = piece.T

    def project(zb):
        rows = xg[pl.ds(zb * 2, 2)].reshape(BLK, D)
        pre = nt(wct[...], rows)
        pret[zb] = pre
        acts = (pre * sigmoid(pre)).astype(BF16)
        actt[zb] = acts
        vrow[zb] = acts[HD:2 * HD].T
        krow[zb] = acts[3 * HD:].T

    def forward_x(s):
        src = ((zh + 4 - s) % 4) * 2 + core
        return copy(xg.at[src], xg.at[src], xfs.at[s], xfr.at[s], mate)

    def arrived_x(s):
        src = ((zh + 4 - s) % 4) * 2 + core
        copy(xg.at[ctx], xg.at[src], xs.at[s], xr.at[s], (dp, ((zh + s) % 4) * 2 + core)).wait_recv()

    send_x[0].wait_recv()
    project(zh)
    for s in (1, 3):
        arrived_x(s)
        forward_x(s).start()
    for s in (1, 3):
        forward_x(s).wait_recv()
        project((zh + 4 - s) % 4)
    arrived_x(2)
    forward_x(2).start()
    forward_x(2).wait_recv()
    project((zh + 2) % 4)

    plane_recv(wb, wrb.at[core], 16)
    send_wo = copy(wrb.at[core], wrb.at[core], wos.at[0], wor.at[0], mate)
    send_wo.start()
    ctv = ct_ref[...]

    l0, l1, l2 = lengths_ref[0, 0], lengths_ref[0, 1], lengths_ref[0, 2]
    e0, e1, e2 = l0, l0 + l1, l0 + l1 + l2

    def pair_of(p):
        i = (p >= 1).astype(jnp.int32) + (p >= 3).astype(jnp.int32) + (p >= 6).astype(jnp.int32)
        return i, p - (i * (i + 1)) // 2

    attt[...] = jnp.zeros_like(attt)

    def forward(p, _):
        i, j = pair_of(p)
        scores = nn(krow[j], actt[i, 2 * HD:3 * HD, :]) * SCALE + toep[i - j]
        qpos = i * BLK + lax.broadcasted_iota(jnp.int32, (1, BLK), 1)
        first = jnp.where(qpos >= e2, e2, jnp.where(qpos >= e1, e1, jnp.where(qpos >= e0, e0, 0)))
        kpos = j * BLK + lax.broadcasted_iota(jnp.int32, (BLK, BLK), 0)
        allowed = (kpos >= first) & (kpos <= qpos)
        sig = sigmoid(scores)
        act = scores * sig
        weights = jnp.where(allowed, act * (1.0 / SEQ), 0.0).astype(BF16)
        wts[p] = weights
        sgs[p] = jnp.where(allowed, (sig + act * (1.0 - sig)) * (1.0 / SEQ), 0.0)
        attt[i] += nn(actt[j, HD:2 * HD, :], weights)
        return 0

    lax.fori_loop(0, PAIRS, forward, 0)

    send_wo.wait_recv()
    dgt = (
        nt(wrb[0].reshape(D, 512), ctv[:, 0:512]) + nt(wrb[1].reshape(D, 512), ctv[:, 512:])
    ).astype(BF16)
    for h in range(HEADS):
        dgs[h] = dgt[h * HD:(h + 1) * HD]

    def ctx_copy(t, src, dst, ss, rs):
        return copy(src, dst, ss.at[t], rs.at[t], (dp, ctx_peer(t)))

    def each(lo, hi, body):
        def step(t, _):
            body(t)
            return 0
        lax.fori_loop(lo, hi, step, 0)

    def from_ctx(t):
        return (ctx + 8 - t) % 8

    each(1, 8, lambda t: ctx_copy(t, dgs.at[ctx_peer(t)], dgr.at[ctx], dss, dsr).start())
    dgr[ctx] = dgs[ctx]
    each(1, 8, lambda t: ctx_copy(t, dgs.at[ctx_peer(t)], dgr.at[from_ctx(t)], dss, dsr).wait_recv())

    def dg_block(b):
        return jnp.concatenate([dgr[2 * b], dgr[2 * b + 1]], axis=1).astype(F32)

    for b in range(NBLK):
        att = attt[b]
        up = dg_block(b) * actt[b, 0:HD, :].astype(F32)
        mean = jnp.sum(att, axis=0, keepdims=True) * (1.0 / HD)
        cen = att - mean
        rows = [
            mean,
            jnp.sum(cen * cen, axis=0, keepdims=True),
            jnp.sum(up, axis=0, keepdims=True),
            jnp.sum(up * cen, axis=0, keepdims=True),
        ]
        stat[b] = jnp.concatenate(rows + [jnp.zeros((4, BLK), F32)], axis=0)
    statr[ctx] = stat[...]
    each(1, 8, lambda t: ctx_copy(t, stat, statr.at[ctx], sts, strr).start())
    each(1, 8, lambda t: ctx_copy(t, stat, statr.at[from_ctx(t)], sts, strr).wait_recv())

    dqt[...] = jnp.zeros_like(dqt)
    dkt[...] = jnp.zeros_like(dkt)
    dvt[...] = jnp.zeros_like(dvt)
    for b in range(NBLK):
        parts = [statr[r, b] for r in range(HEADS)]
        mean = sum([q[0:1] for q in parts]) * (1.0 / HEADS)
        var, s3, s4 = 0.0, 0.0, 0.0
        for q in parts:
            off = q[0:1] - mean
            var = var + q[1:2] + HD * off * off
            s3 = s3 + q[2:3]
            s4 = s4 + q[3:4] + off * q[2:3]
        inv = lax.rsqrt(var * (1.0 / D) + EPSILON)
        m1 = s3 * (1.0 / D)
        m2 = s4 * inv * (1.0 / D)
        norm = (attt[b] - mean) * inv
        dg = dg_block(b)
        u = actt[b, 0:HD, :].astype(F32)
        gated = (norm * u).astype(BF16)
        gts[2 * b] = gated[:, 0:ROWS]
        gts[2 * b + 1] = gated[:, ROWS:]
        dat[b] = ((dg * u - m1 - norm * m2) * inv).astype(BF16)
        uf[b] = dg * norm

    each(1, 8, lambda t: ctx_copy(t, gts.at[ctx_peer(t)], gtr.at[ctx], gss, gsr).start())
    gtr[ctx] = gts[ctx]

    def backward(p, _):
        i, j = pair_of(p)
        da = dat[i]
        ds = (nn(vrow[j], da) * sgs[p]).astype(BF16)
        dqt[i] += nn(actt[j, 3 * HD:, :], ds)
        dkt[j] += nt(actt[i, 2 * HD:3 * HD, :], ds)
        dvt[j] += nt(da, wts[p])
        return 0

    lax.fori_loop(0, PAIRS, backward, 0)

    for b in range(NBLK):
        for part, val in enumerate((uf[b], dvt[b], dqt[b] * SCALE, dkt[b] * SCALE)):
            pre = pret[b, part * HD:(part + 1) * HD, :]
            sig = sigmoid(pre)
            dpt[b, part * HD:(part + 1) * HD, :] = (
                val * (sig * (1.0 + pre * (1.0 - sig)))
            ).astype(BF16)

    def mate_copy(b):
        return copy(pd.at[b], pdr.at[b], pds.at[b], pdsr.at[b], mate)

    for s in (2, 1, 3, 0):
        b = (zh + s) % 4
        col = pl.multiple_of((1 - core) * ROWS, ROWS)
        pd[b] = tn(dpt[b, :, pl.ds(col, ROWS)], wct[...]).astype(BF16)
        mate_copy(b).start()

    def row_copy(s):
        return copy(ps.at[s], pr.at[s], pss.at[s], psr.at[s], (dp, ((zh + s) % 4) * 2 + core))

    for s in (2, 1, 3, 0):
        b = (zh + s) % 4
        col = pl.multiple_of(core * ROWS, ROWS)
        mine = tn(dpt[b, :, pl.ds(col, ROWS)], wct[...])
        mate_copy(b).wait_recv()
        both = mine + pdr[b].astype(F32)
        if s:
            ps[s] = both.astype(BF16)
            row_copy(s).start()
        else:
            own[...] = both

    each(1, 8, lambda t: ctx_copy(t, gts.at[ctx_peer(t)], gtr.at[from_ctx(t)], gss, gsr).wait_recv())
    gt = gtr[...].reshape(D, ROWS)
    for half in range(2):
        cols = slice(half * 512, half * 512 + 512)
        out_ref[:, cols] = (
            x_ref[:, cols].astype(F32) + tn(gt, wrb[half].reshape(D, 512))
        ).astype(BF16)

    def ct_cols(which):
        return jnp.concatenate(
            [ct_ref[:, pl.ds(pl.multiple_of(b * BLK + which * HD, HD), HD)] for b in range(NBLK)], axis=1
        )

    wgd[...] = nn(gt, ct_cols(1 - core)).astype(BF16)
    send_wg = copy(wgd, wgdr, wds.at[0], wdr.at[0], mate)
    send_wg.start()
    wmine = nn(gt, ct_cols(core))
    send_wg.wait_recv()
    wgs[...] = (wmine + wgdr[...].astype(F32)).astype(BF16).reshape(2, PLANE, 32, 512)

    def wg_copy(t, to):
        return copy(
            wgs.at[:, plane_peer(t)], wgr.at[to], wgss.at[t], wgsr.at[t],
            (zl * PLANE + plane_peer(t), ctx),
        )

    each(1, 16, lambda t: wg_copy(t, yx).start())
    wgr[yx] = wgs[:, yx]
    each(1, 16, lambda t: wg_copy(t, plane_from(t)).wait_recv())

    def add_plane(t, total):
        return total + wgr[t].astype(F32)

    wsum = lax.fori_loop(0, PLANE, add_plane, jnp.zeros((2, 32, 512), F32)).astype(BF16)
    for l in range(2):
        for h in range(4):
            wzs[l * 4 + h] = wsum[l, :, h * HD:(h + 1) * HD]

    zat = zl * 4 + zh

    def wz_copy(t, slot):
        to = (zat + t) % 8
        return copy(
            wzs.at[to], wzr.at[slot], wzss.at[t], wzsr.at[t],
            ((to // 4) * PLANE + yx, (to % 4) * 2 + core),
        )

    each(1, 8, lambda t: wz_copy(t, zat).start())
    wzr[zat] = wzs[zat]

    total = own[...]
    for s in (1, 3, 2):
        row_copy(s).wait_recv()
        total = total + pr[s].astype(F32)
    normed, inverse = normalize(x_ref[...].astype(F32))
    first = jnp.mean(total, axis=-1, keepdims=True)
    second = jnp.mean(total * normed, axis=-1, keepdims=True)
    grads_ref[...] = (
        ct_ref[...].astype(F32) + (total - first - normed * second) * inverse
    ).astype(BF16)

    each(1, 8, lambda t: wz_copy(t, (zat + 8 - t) % 8).wait_recv())
    wg_ref[...] = jnp.sum(wzr[...].astype(F32), axis=0)

    send_wa.wait_send()
    send_wb.wait_send()
    for c in send_x:
        c.wait_send()
    for s in (1, 2, 3):
        forward_x(s).wait_send()
        row_copy(s).wait_send()
    plane_done(wa, wra, 0)
    plane_done(wb, wrb.at[core], 16)
    send_wo.wait_send()
    send_wg.wait_send()
    each(1, 8, lambda t: ctx_copy(t, dgs.at[ctx_peer(t)], dgr.at[ctx], dss, dsr).wait_send())
    each(1, 8, lambda t: ctx_copy(t, stat, statr.at[ctx], sts, strr).wait_send())
    each(1, 8, lambda t: ctx_copy(t, gts.at[ctx_peer(t)], gtr.at[ctx], gss, gsr).wait_send())
    for b in range(NBLK):
        mate_copy(b).wait_send()
    each(1, 16, lambda t: wg_copy(t, yx).wait_send())
    each(1, 8, lambda t: wz_copy(t, zat).wait_send())


def on_device(inputs, input_weight, output_weight, cotangent, lengths, buckets, bias_weights):
    vm = lambda *shape, dt=BF16: pltpu.VMEM(shape, dt)
    sem = lambda n: pltpu.SemaphoreType.DMA((n,))
    scratch = [
        vm(8, ROWS, D), vm(2, 32, 512), vm(2, 32, 512),
        vm(2, PLANE, 32, 512), vm(2, 2, PLANE, 32, 512),
        vm(512, D), vm(NBLK, 512, BLK, dt=F32), vm(NBLK, 512, BLK),
        vm(NBLK, BLK, HD), vm(NBLK, BLK, HD),
        vm(PAIRS, BLK, BLK), vm(PAIRS, BLK, BLK, dt=F32), vm(NBLK, BLK, BLK, dt=F32),
        vm(NBLK, HD, BLK, dt=F32), vm(NBLK, HD, BLK, dt=F32),
        vm(8, HD, ROWS), vm(8, HD, ROWS),
        vm(NBLK, 8, BLK, dt=F32), vm(8, NBLK, 8, BLK, dt=F32),
        vm(8, HD, ROWS), vm(8, HD, ROWS), vm(NBLK, HD, BLK),
        vm(NBLK, HD, BLK, dt=F32), vm(NBLK, HD, BLK, dt=F32), vm(NBLK, HD, BLK, dt=F32),
        vm(NBLK, 512, BLK),
        vm(D, 512), vm(D, 512), vm(2, PLANE, 32, 512), vm(PLANE, 2, 32, 512),
        vm(8, 32, HD), vm(8, 32, HD),
        vm(NBLK, ROWS, D), vm(NBLK, ROWS, D), vm(4, ROWS, D), vm(4, ROWS, D), vm(ROWS, D, dt=F32),
        sem(4), sem(4), sem(4), sem(4), sem(2), sem(2), sem(32), sem(32), sem(1), sem(1),
        sem(8), sem(8), sem(8), sem(8), sem(8), sem(8),
        sem(1), sem(1), sem(16), sem(16), sem(8), sem(8), sem(4), sem(4), sem(4), sem(4),
    ]
    vspec = pl.BlockSpec(memory_space=pltpu.VMEM)
    sspec = pl.BlockSpec(memory_space=pltpu.SMEM)
    return pl.pallas_call(
        kernel,
        name="hstu",
        out_shape=(
            jax.ShapeDtypeStruct((ROWS, D), BF16),
            jax.ShapeDtypeStruct((ROWS, D), BF16),
            jax.ShapeDtypeStruct((32, HD), F32),
        ),
        in_specs=[sspec, sspec, vspec, vspec, vspec, vspec, vspec],
        out_specs=(vspec, vspec, vspec),
        scratch_shapes=scratch,
        compiler_params=pltpu.CompilerParams(
            collective_id=0, has_side_effects=True, vmem_limit_bytes=56 << 20
        ),
    )(lengths, bias_weights, buckets.reshape(1, SEQ), inputs, input_weight, output_weight, cotangent)


def solution(mesh):
    return jax.shard_map(
        on_device,
        mesh=mesh,
        in_specs=(
            P(("dp", "ctx"), None),
            P("dp", None),
            P("dp", None),
            P(("dp", "ctx"), None),
            P("dp", None),
            P(),
            P(),
        ),
        out_specs=(P(("dp", "ctx"), None), P(("dp", "ctx"), None), P("dp", "ctx")),
        check_vma=False,
    )
```

```python
import functools
import math

import jax
import jax.numpy as jnp
from jax import lax
from jax.experimental import pallas as pl
from jax.experimental.pallas import tpu as pltpu
from jax.sharding import PartitionSpec as P

EPSILON = 1e-06
MESH = pl.DeviceIdType.MESH
F32 = jnp.float32
BF16 = jnp.bfloat16

ROWS = 128
BLK = 256
NBLK = 4
HEADS = 8
HD = 128
D = 1024
SEQ = 1024
PLANE = 16
PAIRS = NBLK * (NBLK + 1) // 2
SCALE = 1.0 / math.sqrt(HD)


def nn(a, b):
    return lax.dot_general(a, b, (((1,), (0,)), ((), ())), preferred_element_type=F32)


def nt(a, b):
    return lax.dot_general(a, b, (((1,), (1,)), ((), ())), preferred_element_type=F32)


def tn(a, b):
    return lax.dot_general(a, b, (((0,), (0,)), ((), ())), preferred_element_type=F32)


def sigmoid(values):
    return 0.5 * jnp.tanh(0.5 * values) + 0.5


def normalize(values):
    average = jnp.mean(values, axis=-1, keepdims=True)
    centered = values - average
    inverse = lax.rsqrt(jnp.mean(centered * centered, axis=-1, keepdims=True) + EPSILON)
    return (centered * inverse, inverse)


def kernel(
    lengths_ref, bias_ref, buckets_ref, x_ref, win_ref, wout_ref, ct_ref,
    out_ref, grads_ref, wg_ref,
    xg, wa, wb, wra, wrb, wct, pret, actt, krow, vrow, wts, sgs, toep, attt, uf,
    dgs, dgr, stat, statr, gts, gtr, dat, dqt, dkt, dvt, dpt,
    wgd, wgdr, wgs, wgr, wzs, wzr,
    pd, pdr, ps, pr, own,
    xs, xr, xfs, xfr, was, war, wps, wpr, wos, wor, dss, dsr, sts, strr, gss, gsr,
    wds, wdr, wgss, wgsr, wzss, wzsr, pds, pdsr, pss, psr,
):
    dp = lax.axis_index("dp")
    ctx = lax.axis_index("ctx")
    zh, core = ctx // 2, ctx % 2
    zl, yx = dp // PLANE, dp % PLANE
    y, x = yx // 4, yx % 4
    mate = (dp, zh * 2 + 1 - core)

    def ctx_peer(t):
        return (ctx + t) % 8

    def plane_peer(t):
        return ((y + t // 4) % 4) * 4 + (x + t % 4) % 4

    def plane_from(t):
        return ((y + 4 - t // 4) % 4) * 4 + (x + 4 - t % 4) % 4

    started = []

    class Copies:
        def __init__(self, make, lo=0, hi=1):
            self.make, self.lo, self.hi, self.received = make, lo, hi, False

        def each(self, act, landed=False):
            def one(t, _):
                src, dst, ss, rs, dev = self.make(t, landed)
                act(
                    pltpu.make_async_remote_copy(
                        src_ref=src, dst_ref=dst, send_sem=ss, recv_sem=rs,
                        device_id=dev, device_id_type=MESH,
                    )
                )
                return 0

            if self.hi - self.lo == 1:
                one(self.lo, 0)
            else:
                lax.fori_loop(self.lo, self.hi, one, 0)

        def start(self):
            started.append(self)
            self.each(lambda c: c.start())
            return self

        def wait(self):
            self.received = True
            self.each(lambda c: c.wait_recv(), True)

        def sent(self):
            self.each(lambda c: c.wait_send())

    def finish():
        for c in started:
            if not c.received:
                c.wait()
        for c in started:
            c.sent()

    barrier = pltpu.get_barrier_semaphore()

    def greet_ctx(t, _):
        pl.semaphore_signal(barrier, inc=1, device_id=(dp, ctx_peer(t)), device_id_type=MESH)
        return 0

    def greet_plane(t, _):
        pl.semaphore_signal(
            barrier, inc=1, device_id=(zl * PLANE + plane_peer(t), ctx), device_id_type=MESH
        )
        return 0

    def greet_column(t, _):
        pl.semaphore_signal(
            barrier, inc=1, device_id=((1 - zl) * PLANE + yx, t * 2 + core), device_id_type=MESH
        )
        return 0

    lax.fori_loop(1, 8, greet_ctx, 0)
    lax.fori_loop(1, 16, greet_plane, 0)
    lax.fori_loop(0, 4, greet_column, 0)

    normed, _ = normalize(x_ref[...].astype(F32))
    xg[ctx] = normed.astype(BF16)
    for part in range(4):
        at = pl.multiple_of(part * D + ctx * HD, HD)
        wa[zl, :, part * HD:(part + 1) * HD] = win_ref[:, pl.ds(at, HD)]
    wb[zl] = wout_ref[:, pl.ds(pl.multiple_of(core * 512, 512), 512)]

    pl.semaphore_wait(barrier, 26)

    other = ((1 - zl) * PLANE + yx, ctx)

    def across(ref, k):
        return Copies(lambda t, landed: (
            ref.at[zl], ref.at[1 - zl if landed else zl], was.at[k], war.at[k], other))

    def half_rows(r, h):
        return xg.at[r, pl.ds(h * 64, 64)]

    def own_rows(s, h):
        src = ((zh + 4 - s) % 4) * 2 + core
        return Copies(lambda t, landed: (
            half_rows(ctx, h), half_rows(src if landed else ctx, h), xs.at[s * 2 + h], xr.at[s * 2 + h],
            (dp, ((zh + s) % 4) * 2 + core)))

    def relayed_rows(s, h):
        src = ((zh + 4 - s) % 4) * 2 + core
        far = ((zh + 2) % 4) * 2 + core
        return Copies(lambda t, landed: (
            half_rows(src, h), half_rows(far if landed else src, h), xs.at[4 + h], xr.at[4 + h],
            (dp, ((zh + s) % 4) * 2 + core)))

    def mate_rows(s, h):
        chip = ((zh + 4 - s) % 4) * 2
        return Copies(lambda t, landed: (
            half_rows(chip + core, h), half_rows(chip + (1 - core if landed else core), h),
            xfs.at[s * 2 + h], xfr.at[s * 2 + h], mate))

    def over_plane(src, dst, l, base):
        return Copies(lambda t, landed: (
            src.at[l], dst.at[l, plane_from(t) if landed else yx], wps.at[base + t], wpr.at[base + t],
            (zl * PLANE + plane_peer(t), ctx)), 1, PLANE)

    def from_ctx(t):
        return (ctx + 8 - t) % 8

    def all_to_all(src, dst, ss, rs):
        return Copies(lambda t, landed: (
            src.at[ctx_peer(t)], dst.at[from_ctx(t) if landed else ctx], ss.at[t], rs.at[t],
            (dp, ctx_peer(t))), 1, 8)

    xb = across(wb, 1).start()
    xa = across(wa, 0).start()
    to_mate_rows = [[None, None] for _ in range(4)]
    for h in range(2):
        to_mate_rows[0][h] = mate_rows(0, h).start()
    up0, down1 = own_rows(1, 0).start(), own_rows(3, 1).start()
    up1, down0 = own_rows(1, 1).start(), own_rows(3, 0).start()
    out_own = over_plane(wb, wrb.at[core], zl, 0).start()
    in_own = over_plane(wa, wra, zl, 32).start()

    buckets = buckets_ref[...]
    table = jnp.zeros((1, SEQ), F32)
    for b in range(32):
        table = jnp.where(buckets == b, bias_ref[ctx, b], table)
    padded = jnp.concatenate([table[:, 0:BLK], table], axis=1)
    for d in range(NBLK):
        wide = jnp.broadcast_to(padded[:, d * BLK:d * BLK + 2 * BLK], (BLK, 2 * BLK))
        toep[d] = pltpu.roll(wide, 0, 1, stride=1, stride_axis=0)[:, BLK:]

    xb.wait()
    out_other = over_plane(wb, wrb.at[core], 1 - zl, 16).start()
    wrb[core, :, yx] = wb[...]
    xa.wait()
    in_other = over_plane(wa, wra, 1 - zl, 48).start()
    wra[:, yx] = wa[...]

    up0.wait()
    far0 = relayed_rows(1, 0).start()
    to_mate_rows[1][0] = mate_rows(1, 0).start()
    down1.wait()
    far1 = relayed_rows(3, 1).start()
    to_mate_rows[3][1] = mate_rows(3, 1).start()
    up1.wait()
    to_mate_rows[1][1] = mate_rows(1, 1).start()
    down0.wait()
    to_mate_rows[3][0] = mate_rows(3, 0).start()

    out_own.wait()
    out_other.wait()
    mates_half = Copies(lambda t, landed: (
        wrb.at[core], wrb.at[1 - core if landed else core], wos.at[0], wor.at[0], mate)).start()
    in_own.wait()
    in_other.wait()
    mates_half.wait()
    ctv = ct_ref[...]
    dgt = (
        nt(wrb[0].reshape(D, 512), ctv[:, 0:512]) + nt(wrb[1].reshape(D, 512), ctv[:, 512:])
    ).astype(BF16)
    for h in range(HEADS):
        dgs[h] = dgt[h * HD:(h + 1) * HD]
    dg_sent = all_to_all(dgs, dgr, dss, dsr).start()
    dgr[ctx] = dgs[ctx]

    for part in range(4):
        piece = wra[:, :, :, part * HD:(part + 1) * HD].reshape(D, HD)
        wct[part * HD:(part + 1) * HD, :] = piece.T

    def project(zb):
        rows = xg[pl.ds(zb * 2, 2)].reshape(BLK, D)
        pre = nt(wct[...], rows)
        pret[zb] = pre
        acts = (pre * sigmoid(pre)).astype(BF16)
        actt[zb] = acts
        vrow[zb] = acts[HD:2 * HD].T
        krow[zb] = acts[3 * HD:].T

    for s in (0, 1, 3):
        for h in range(2):
            to_mate_rows[s][h].wait()
        project((zh + 4 - s) % 4)
    far0.wait()
    to_mate_rows[2][0] = mate_rows(2, 0).start()
    far1.wait()
    to_mate_rows[2][1] = mate_rows(2, 1).start()
    for h in range(2):
        to_mate_rows[2][h].wait()
    project((zh + 2) % 4)

    l0, l1, l2 = lengths_ref[0, 0], lengths_ref[0, 1], lengths_ref[0, 2]
    e0, e1, e2 = l0, l0 + l1, l0 + l1 + l2

    def pair_of(p):
        i = (p >= 1).astype(jnp.int32) + (p >= 3).astype(jnp.int32) + (p >= 6).astype(jnp.int32)
        return i, p - (i * (i + 1)) // 2

    def dg_block(b):
        return jnp.concatenate([dgr[2 * b], dgr[2 * b + 1]], axis=1).astype(F32)

    def forward(i):
        qpos = i * BLK + lax.broadcasted_iota(jnp.int32, (1, BLK), 1)
        first = jnp.where(qpos >= e2, e2, jnp.where(qpos >= e1, e1, jnp.where(qpos >= e0, e0, 0)))
        att = jnp.zeros((HD, BLK), F32)
        for j in range(i + 1):
            p = i * (i + 1) // 2 + j
            scores = nn(krow[j], actt[i, 2 * HD:3 * HD, :]) * SCALE + toep[i - j]
            kpos = j * BLK + lax.broadcasted_iota(jnp.int32, (BLK, BLK), 0)
            allowed = kpos >= first
            if i == j:
                allowed = allowed & (kpos <= qpos)
            sig = sigmoid(scores)
            act = scores * sig
            weights = jnp.where(allowed, act * (1.0 / SEQ), 0.0).astype(BF16)
            wts[p] = weights
            sgs[p] = jnp.where(allowed, (sig + act * (1.0 - sig)) * (1.0 / SEQ), 0.0)
            att = att + nn(actt[j, HD:2 * HD, :], weights)
        attt[i] = att

    def statistics(b):
        att = attt[b]
        up = dg_block(b) * actt[b, 0:HD, :].astype(F32)
        mean = jnp.sum(att, axis=0, keepdims=True) * (1.0 / HD)
        cen = att - mean
        rows = [
            mean,
            jnp.sum(cen * cen, axis=0, keepdims=True),
            jnp.sum(up, axis=0, keepdims=True),
            jnp.sum(up * cen, axis=0, keepdims=True),
        ]
        stat[b] = jnp.concatenate([q[:, :ROWS] for q in rows] + [q[:, ROWS:] for q in rows], axis=0)
        statr[b, ctx] = stat[b]
        return Copies(lambda t, landed: (
            stat.at[b], statr.at[b, from_ctx(t) if landed else ctx], sts.at[b * 8 + t], strr.at[b * 8 + t],
            (dp, ctx_peer(t))), 1, 8).start()

    stats_sent = {}
    for b in (3, 2, 1, 0):
        forward(b)
        if b == 3:
            dg_sent.wait()
        stats_sent[b] = statistics(b)

    dqt[...] = jnp.zeros_like(dqt)
    dkt[...] = jnp.zeros_like(dkt)
    dvt[...] = jnp.zeros_like(dvt)
    def combined(b):
        stats_sent[b].wait()
        parts = [
            jnp.concatenate([statr[b, r, 0:4], statr[b, r, 4:8]], axis=1) for r in range(HEADS)
        ]
        mean = sum([q[0:1] for q in parts]) * (1.0 / HEADS)
        var, s3, s4 = 0.0, 0.0, 0.0
        for q in parts:
            off = q[0:1] - mean
            var = var + q[1:2] + HD * off * off
            s3 = s3 + q[2:3]
            s4 = s4 + q[3:4] + off * q[2:3]
        inv = lax.rsqrt(var * (1.0 / D) + EPSILON)
        m1 = s3 * (1.0 / D)
        m2 = s4 * inv * (1.0 / D)
        norm = (attt[b] - mean) * inv
        dg = dg_block(b)
        u = actt[b, 0:HD, :].astype(F32)
        gated = (norm * u).astype(BF16)
        gts[2 * b] = gated[:, 0:ROWS]
        gts[2 * b + 1] = gated[:, ROWS:]
        dat[b] = ((dg * u - m1 - norm * m2) * inv).astype(BF16)
        uf[b] = dg * norm

    for b in (3, 2, 1, 0):
        combined(b)
    gated_sent = all_to_all(gts, gtr, gss, gsr).start()
    gtr[ctx] = gts[ctx]

    def backward(p, _):
        i, j = pair_of(p)
        da = dat[i]
        ds = (nn(vrow[j], da) * sgs[p]).astype(BF16)
        dqt[i] += nn(actt[j, 3 * HD:, :], ds)
        dkt[j] += nt(actt[i, 2 * HD:3 * HD, :], ds)
        dvt[j] += nt(da, wts[p])
        return 0

    lax.fori_loop(0, PAIRS, backward, 0)

    for b in range(NBLK):
        for part, val in enumerate((uf[b], dvt[b], dqt[b] * SCALE, dkt[b] * SCALE)):
            pre = pret[b, part * HD:(part + 1) * HD, :]
            sig = sigmoid(pre)
            dpt[b, part * HD:(part + 1) * HD, :] = (
                val * (sig * (1.0 + pre * (1.0 - sig)))
            ).astype(BF16)

    def to_mate(b):
        return Copies(lambda t, landed: (pd.at[b], pdr.at[b], pds.at[b], pdsr.at[b], mate))

    mates = {}
    for s in (2, 1, 3, 0):
        b = (zh + s) % 4
        col = pl.multiple_of((1 - core) * ROWS, ROWS)
        pd[b] = tn(dpt[b, :, pl.ds(col, ROWS)], wct[...]).astype(BF16)
        mates[s] = to_mate(b).start()

    def to_owner(s):
        return Copies(lambda t, landed: (
            ps.at[s], pr.at[s], pss.at[s], psr.at[s], (dp, ((zh + s) % 4) * 2 + core)))

    owners = {}

    for s in (2, 1, 3, 0):
        b = (zh + s) % 4
        col = pl.multiple_of(core * ROWS, ROWS)
        mine = tn(dpt[b, :, pl.ds(col, ROWS)], wct[...])
        mates[s].wait()
        both = mine + pdr[b].astype(F32)
        if s:
            ps[s] = both.astype(BF16)
            owners[s] = to_owner(s).start()
        else:
            own[...] = both

    gated_sent.wait()
    gt = gtr[...].reshape(D, ROWS)
    for half in range(2):
        cols = slice(half * 512, half * 512 + 512)
        out_ref[:, cols] = (
            x_ref[:, cols].astype(F32) + tn(gt, wrb[half].reshape(D, 512))
        ).astype(BF16)

    def ct_cols(which):
        return jnp.concatenate(
            [ct_ref[:, pl.ds(pl.multiple_of(b * BLK + which * HD, HD), HD)] for b in range(NBLK)], axis=1
        )

    wgd[...] = nn(gt, ct_cols(1 - core)).astype(BF16)
    wg_mate = Copies(lambda t, landed: (wgd, wgdr, wds.at[0], wdr.at[0], mate)).start()
    wmine = nn(gt, ct_cols(core))
    wg_mate.wait()
    wgs[...] = (wmine + wgdr[...].astype(F32)).astype(BF16).reshape(2, PLANE, 32, 512)

    wg_plane = Copies(lambda t, landed: (
        wgs.at[:, plane_peer(t)], wgr.at[plane_from(t) if landed else yx], wgss.at[t], wgsr.at[t],
        (zl * PLANE + plane_peer(t), ctx)), 1, PLANE).start()
    wgr[yx] = wgs[:, yx]
    wg_plane.wait()

    def add_plane(t, total):
        return total + wgr[t].astype(F32)

    wsum = lax.fori_loop(0, PLANE, add_plane, jnp.zeros((2, 32, 512), F32)).astype(BF16)
    for l in range(2):
        for h in range(4):
            wzs[l * 4 + h] = wsum[l, :, h * HD:(h + 1) * HD]

    zat = zl * 4 + zh

    def column(t, landed):
        to = (zat + t) % 8
        return (
            wzs.at[to], wzr.at[(zat + 8 - t) % 8 if landed else zat], wzss.at[t], wzsr.at[t],
            ((to // 4) * PLANE + yx, (to % 4) * 2 + core),
        )

    wg_column = Copies(column, 1, 8).start()
    wzr[zat] = wzs[zat]

    total = own[...]
    for s in (1, 3, 2):
        owners[s].wait()
        total = total + pr[s].astype(F32)
    normed, inverse = normalize(x_ref[...].astype(F32))
    first = jnp.mean(total, axis=-1, keepdims=True)
    second = jnp.mean(total * normed, axis=-1, keepdims=True)
    grads_ref[...] = (
        ct_ref[...].astype(F32) + (total - first - normed * second) * inverse
    ).astype(BF16)

    wg_column.wait()
    wg_ref[...] = jnp.sum(wzr[...].astype(F32), axis=0)

    finish()


def on_device(inputs, input_weight, output_weight, cotangent, lengths, buckets, bias_weights):
    vm = lambda *shape, dt=BF16: pltpu.VMEM(shape, dt)
    sem = lambda n: pltpu.SemaphoreType.DMA((n,))
    scratch = [
        vm(8, ROWS, D), vm(2, 32, 512), vm(2, 32, 512),
        vm(2, PLANE, 32, 512), vm(2, 2, PLANE, 32, 512),
        vm(512, D), vm(NBLK, 512, BLK, dt=F32), vm(NBLK, 512, BLK),
        vm(NBLK, BLK, HD), vm(NBLK, BLK, HD),
        vm(PAIRS, BLK, BLK), vm(PAIRS, BLK, BLK, dt=F32), vm(NBLK, BLK, BLK, dt=F32),
        vm(NBLK, HD, BLK, dt=F32), vm(NBLK, HD, BLK, dt=F32),
        vm(8, HD, ROWS), vm(8, HD, ROWS),
        vm(NBLK, 8, HD, dt=F32), vm(NBLK, 8, 8, HD, dt=F32),
        vm(8, HD, ROWS), vm(8, HD, ROWS), vm(NBLK, HD, BLK),
        vm(NBLK, HD, BLK, dt=F32), vm(NBLK, HD, BLK, dt=F32), vm(NBLK, HD, BLK, dt=F32),
        vm(NBLK, 512, BLK),
        vm(D, 512), vm(D, 512), vm(2, PLANE, 32, 512), vm(PLANE, 2, 32, 512),
        vm(8, 32, HD), vm(8, 32, HD),
        vm(NBLK, ROWS, D), vm(NBLK, ROWS, D), vm(4, ROWS, D), vm(4, ROWS, D), vm(ROWS, D, dt=F32),
        sem(8), sem(8), sem(8), sem(8), sem(2), sem(2), sem(64), sem(64), sem(1), sem(1),
        sem(8), sem(8), sem(32), sem(32), sem(8), sem(8),
        sem(1), sem(1), sem(16), sem(16), sem(8), sem(8), sem(4), sem(4), sem(4), sem(4),
    ]
    vspec = pl.BlockSpec(memory_space=pltpu.VMEM)
    sspec = pl.BlockSpec(memory_space=pltpu.SMEM)
    return pl.pallas_call(
        kernel,
        name="hstu",
        out_shape=(
            jax.ShapeDtypeStruct((ROWS, D), BF16),
            jax.ShapeDtypeStruct((ROWS, D), BF16),
            jax.ShapeDtypeStruct((32, HD), F32),
        ),
        in_specs=[sspec, sspec, vspec, vspec, vspec, vspec, vspec],
        out_specs=(vspec, vspec, vspec),
        scratch_shapes=scratch,
        compiler_params=pltpu.CompilerParams(
            collective_id=0, has_side_effects=True, vmem_limit_bytes=56 << 20
        ),
    )(lengths, bias_weights, buckets.reshape(1, SEQ), inputs, input_weight, output_weight, cotangent)


def solution(mesh):
    return jax.shard_map(
        on_device,
        mesh=mesh,
        in_specs=(
            P(("dp", "ctx"), None),
            P("dp", None),
            P("dp", None),
            P(("dp", "ctx"), None),
            P("dp", None),
            P(),
            P(),
        ),
        out_specs=(P(("dp", "ctx"), None), P(("dp", "ctx"), None), P("dp", "ctx")),
        check_vma=False,
    )
```

```python
import functools
import math

import jax
import jax.numpy as jnp
from jax import lax
from jax.experimental import pallas as pl
from jax.experimental.pallas import tpu as pltpu
from jax.sharding import PartitionSpec as P

EPSILON = 1e-06
MESH = pl.DeviceIdType.MESH
F32 = jnp.float32
BF16 = jnp.bfloat16

ROWS = 128
BLK = 256
NBLK = 4
HEADS = 8
HD = 128
D = 1024
SEQ = 1024
PLANE = 16
PAIRS = NBLK * (NBLK + 1) // 2
SCALE = 1.0 / math.sqrt(HD)


def nn(a, b):
    return lax.dot_general(a, b, (((1,), (0,)), ((), ())), preferred_element_type=F32)


def nt(a, b):
    return lax.dot_general(a, b, (((1,), (1,)), ((), ())), preferred_element_type=F32)


def tn(a, b):
    return lax.dot_general(a, b, (((0,), (0,)), ((), ())), preferred_element_type=F32)


def sigmoid(values):
    return 0.5 * jnp.tanh(0.5 * values) + 0.5


def normalize(values):
    average = jnp.mean(values, axis=-1, keepdims=True)
    centered = values - average
    inverse = lax.rsqrt(jnp.mean(centered * centered, axis=-1, keepdims=True) + EPSILON)
    return (centered * inverse, inverse)


def kernel(
    lengths_ref, bias_ref, buckets_ref, x_ref, win_ref, wout_ref, ct_ref,
    out_ref, grads_ref, wg_ref,
    xg, wa, wb, wbo, wra, wrb, wct, pret, actt, krow, vrow, wts, sgs, toep, attt, uf,
    dgs, dgr, stat, statr, ats, atr, uts, utr, gto, gtm, ctc, xv, dat, dkt, dvt, dpt,
    wgs, wgr, wzs, wzr,
    pd, pdr, pm, ps, pr, rr, own,
    xs, xr, xfs, xfr, was, war, wps, wpr, wos, wor, dss, dsr, sts, strr, gss, gsr,
    wds, wdr, wgss, wgsr, wzss, wzsr, pds, pdsr, pss, psr, uss, usr, lds,
):
    dp = lax.axis_index("dp")
    ctx = lax.axis_index("ctx")
    zh, core = ctx // 2, ctx % 2
    zl, yx = dp // PLANE, dp % PLANE
    y, x = yx // 4, yx % 4
    mate = (dp, zh * 2 + 1 - core)

    def ctx_peer(t):
        return (ctx + t) % 8

    def plane_peer(t):
        return ((y + t // 4) % 4) * 4 + (x + t % 4) % 4

    def plane_from(t):
        return ((y + 4 - t // 4) % 4) * 4 + (x + 4 - t % 4) % 4

    started = []

    class Copies:
        def __init__(self, make, lo=0, hi=1, where=None):
            self.make, self.lo, self.hi, self.where, self.received = make, lo, hi, where, False

        def each(self, act, landed=False):
            def one(t, _):
                if self.where is None:
                    run(t)
                else:
                    pl.when(self.where(t, landed))(lambda: run(t))
                return 0

            def run(t):
                src, dst, ss, rs, dev = self.make(t, landed)
                act(
                    pltpu.make_async_remote_copy(
                        src_ref=src, dst_ref=dst, send_sem=ss, recv_sem=rs,
                        device_id=dev, device_id_type=MESH,
                    )
                )

            if self.hi - self.lo == 1:
                one(self.lo, 0)
            else:
                lax.fori_loop(self.lo, self.hi, one, 0)

        def go(self):
            self.each(lambda c: c.start())

        def start(self):
            started.append(self)
            self.go()
            return self

        def wait(self):
            self.received = True
            self.each(lambda c: c.wait_recv(), True)

        def sent(self):
            self.each(lambda c: c.wait_send())

    def finish():
        for c in started:
            if not c.received:
                c.wait()
        for c in started:
            c.sent()

    barrier = pltpu.get_barrier_semaphore()

    def greet_ctx(t, _):
        pl.semaphore_signal(barrier, inc=1, device_id=(dp, ctx_peer(t)), device_id_type=MESH)
        return 0

    def greet_plane(t, _):
        pl.semaphore_signal(
            barrier, inc=1, device_id=(zl * PLANE + plane_peer(t), ctx), device_id_type=MESH
        )
        return 0

    def greet_column(t, _):
        pl.semaphore_signal(
            barrier, inc=1, device_id=((1 - zl) * PLANE + yx, t * 2 + core), device_id_type=MESH
        )
        return 0

    lax.fori_loop(1, 8, greet_ctx, 0)
    lax.fori_loop(1, 16, greet_plane, 0)
    lax.fori_loop(0, 4, greet_column, 0)

    load_x = pltpu.make_async_copy(x_ref, xv, lds.at[0])
    load_x.start()
    load_w = [
        pltpu.make_async_copy(wout_ref, wbo, lds.at[1])
    ]
    for part in range(4):
        at = pl.multiple_of(part * D + ctx * HD, HD)
        load_w.append(
            pltpu.make_async_copy(
                win_ref.at[:, pl.ds(at, HD)], wa.at[zl, :, pl.ds(part * HD, HD)], lds.at[2 + part]
            )
        )
    for c in load_w:
        c.start()
    load_ct = pltpu.make_async_copy(ct_ref, ctc.at[core], lds.at[6])
    load_ct.start()
    load_x.wait()
    normed, _ = normalize(xv[...].astype(F32))
    xg[ctx] = normed.astype(BF16)
    for c in load_w:
        c.wait()

    pl.semaphore_wait(barrier, 26)

    other = ((1 - zl) * PLANE + yx, ctx)

    def across(ref, k):
        return Copies(lambda t, landed: (
            ref.at[zl], ref.at[1 - zl if landed else zl], was.at[k], war.at[k], other))

    def half_rows(r, h):
        return xg.at[r, pl.ds(h * 64, 64)]

    def own_rows(s, h):
        src = ((zh + 4 - s) % 4) * 2 + core
        return Copies(lambda t, landed: (
            half_rows(ctx, h), half_rows(src if landed else ctx, h), xs.at[s * 2 + h], xr.at[s * 2 + h],
            (dp, ((zh + s) % 4) * 2 + core)))

    def relayed_rows(s, h):
        src = ((zh + 4 - s) % 4) * 2 + core
        far = ((zh + 2) % 4) * 2 + core
        return Copies(lambda t, landed: (
            half_rows(src, h), half_rows(far if landed else src, h), xs.at[4 + h], xr.at[4 + h],
            (dp, ((zh + s) % 4) * 2 + core)))

    def mate_rows(s, h):
        chip = ((zh + 4 - s) % 4) * 2
        return Copies(lambda t, landed: (
            half_rows(chip + core, h), half_rows(chip + (1 - core if landed else core), h),
            xfs.at[s * 2 + h], xfr.at[s * 2 + h], mate))

    def step_by(axis, ty, tx, t):
        return (ty, (tx + t) % 4) if axis == "x" else ((ty + t) % 4, tx)

    def in_plane(place):
        return (zl * PLANE + place[0] * 4 + place[1], ctx)

    class Spread:
        def __init__(self, src, dst, axis, base):
            self.src, self.dst, self.axis, self.base = src, dst, axis, base
            self.cross = "y" if axis == "x" else "x"
            self.first, self.rest = [], []

        def own(self):
            for axis in (self.axis, self.cross):
                for t in (1, 3, 2):
                    at = self.base + (axis == self.cross) * 3 + t - 1

                    def make(_, landed, axis=axis, t=t, at=at):
                        py, px = step_by(axis, y, x, 4 - t) if landed else (y, x)
                        return (self.src, self.dst(py, px), wps.at[at], wpr.at[at],
                                in_plane(step_by(axis, y, x, t)))

                    (self.first if axis == self.axis else self.rest).append(Copies(make).start())

        def hand_on(self):
            for n, t in enumerate((1, 3, 2)):
                self.first[n].wait()
                for u in (1, 3, 2):
                    at = self.base + 6 + (t - 1) * 3 + u - 1

                    def make(_, landed, t=t, u=u, at=at):
                        py, px = step_by(self.axis, y, x, 4 - t)
                        ty, tx = step_by(self.cross, py, px, 4 - u) if landed else (py, px)
                        return (self.dst(py, px), self.dst(ty, tx), wps.at[at], wpr.at[at],
                                in_plane(step_by(self.cross, y, x, u)))

                    self.rest.append(Copies(make).start())

        def wait(self):
            for c in self.rest:
                c.wait()

    def from_ctx(t):
        return (ctx + 8 - t) % 8

    def all_to_all(src, dst, ss, rs):
        return Copies(lambda t, landed: (
            src.at[ctx_peer(t)], dst.at[from_ctx(t) if landed else ctx], ss.at[t], rs.at[t],
            (dp, ctx_peer(t))), 1, 8)

    mine_b = zl == core
    xb = Copies(lambda t, landed: (wbo, wb, was.at[1], war.at[1], other), where=lambda t, landed: (
        jnp.logical_not(mine_b) if landed else mine_b)).start()
    xa = across(wa, 0).start()
    to_mate_rows = [[None, None] for _ in range(4)]
    for h in range(2):
        to_mate_rows[0][h] = mate_rows(0, h).start()
    up0, down1 = own_rows(1, 0).start(), own_rows(3, 1).start()
    up1, down0 = own_rows(1, 1).start(), own_rows(3, 0).start()
    @pl.when(mine_b)
    def _():
        wb[...] = wbo[...]

    xb.wait()
    lo, hi = pl.ds(0, 512), pl.ds(512, 512)
    out_spread = [
        Spread(wb.at[:, lo], lambda py, px: wrb.at[core, py, px, :, lo], "x", 0),
        Spread(wb.at[:, hi], lambda py, px: wrb.at[core, py, px, :, hi], "y", 16),
    ]
    for w in out_spread:
        w.own()
    load_ct.wait()
    ct_mate = Copies(lambda t, landed: (
        ctc.at[core], ctc.at[1 - core if landed else core], wds.at[0], wdr.at[0], mate)).start()
    xa.wait()
    low, high = pl.ds(0, 256), pl.ds(256, 256)
    in_spread = [
        Spread(wa.at[:, :, low], lambda py, px: wra.at[:, py, px, :, low], "x", 32),
        Spread(wa.at[:, :, high], lambda py, px: wra.at[:, py, px, :, high], "y", 48),
    ]
    for w in in_spread:
        w.own()
    wrb[core, y, x] = wb[...]
    wra[:, y, x] = wa[...]
    for w in out_spread:
        w.hand_on()

    buckets = buckets_ref[...]
    table = jnp.zeros((1, SEQ), F32)
    for b in range(32):
        table = jnp.where(buckets == b, bias_ref[ctx, b], table)
    padded = jnp.concatenate([table[:, 0:BLK], table], axis=1)
    for d in range(NBLK):
        wide = jnp.broadcast_to(padded[:, d * BLK:d * BLK + 2 * BLK], (BLK, 2 * BLK))
        toep[d] = pltpu.roll(wide, 0, 1, stride=1, stride_axis=0)[:, BLK:]

    up0.wait()
    far0 = relayed_rows(1, 0).start()
    to_mate_rows[1][0] = mate_rows(1, 0).start()
    down1.wait()
    far1 = relayed_rows(3, 1).start()
    to_mate_rows[3][1] = mate_rows(3, 1).start()
    up1.wait()
    to_mate_rows[1][1] = mate_rows(1, 1).start()
    down0.wait()
    to_mate_rows[3][0] = mate_rows(3, 0).start()

    for w in in_spread:
        w.hand_on()

    for w in out_spread:
        w.wait()
    ct_mate.wait()
    ct_chip = ctc[...].reshape(BLK, D)
    wout_half = wrb[core].reshape(512, D)
    for n in range(4):
        dgs[n] = nt(wout_half[n * HD:(n + 1) * HD], ct_chip).astype(BF16)

    def head_at(n):
        return core * 4 + n

    from_half = zh // 2
    dg_sent = Copies(
        lambda t, landed: (
            dgs.at[t], dgr.at[t if landed else zh], dss.at[t], dsr.at[t if landed else zh], (dp, head_at(t))),
        0, 4,
        where=lambda t, landed: (t * 2 + from_half != ctx) if landed else (head_at(t) != ctx),
    ).start()

    @pl.when(from_half == core)
    def _():
        dgr[zh] = dgs[ctx % 4]

    mates_half = Copies(lambda t, landed: (
        wrb.at[core], wrb.at[1 - core if landed else core], wos.at[0], wor.at[0], mate)).start()

    for w in in_spread:
        w.wait()
    for part in range(4):
        piece = wra[:, :, :, :, part * HD:(part + 1) * HD].reshape(D, HD)
        wct[part * HD:(part + 1) * HD, :] = piece.T

    def project(zb):
        rows = xg[pl.ds(zb * 2, 2)].reshape(BLK, D)
        pre = nt(wct[...], rows)
        pret[zb] = pre
        acts = (pre * sigmoid(pre)).astype(BF16)
        actt[zb] = acts
        vrow[zb] = acts[HD:2 * HD].T
        krow[zb] = acts[3 * HD:].T

    for s in (0, 1, 3):
        for h in range(2):
            to_mate_rows[s][h].wait()
        project((zh + 4 - s) % 4)
    far0.wait()
    to_mate_rows[2][0] = mate_rows(2, 0).start()
    far1.wait()
    to_mate_rows[2][1] = mate_rows(2, 1).start()
    for h in range(2):
        to_mate_rows[2][h].wait()
    project((zh + 2) % 4)

    for b in range(NBLK):
        uts[2 * b] = actt[b, 0:HD, 0:ROWS]
        uts[2 * b + 1] = actt[b, 0:HD, ROWS:]
    u_sent = all_to_all(uts, utr, uss, usr).start()
    utr[ctx] = uts[ctx]

    l0, l1, l2 = lengths_ref[0, 0], lengths_ref[0, 1], lengths_ref[0, 2]
    e0, e1, e2 = l0, l0 + l1, l0 + l1 + l2

    def forward(i):
        qpos = i * BLK + lax.broadcasted_iota(jnp.int32, (1, BLK), 1)
        first = jnp.where(qpos >= e2, e2, jnp.where(qpos >= e1, e1, jnp.where(qpos >= e0, e0, 0)))
        att = jnp.zeros((HD, BLK), F32)
        for j in range(i + 1):
            p = i * (i + 1) // 2 + j
            scores = nn(krow[j], actt[i, 2 * HD:3 * HD, :]) * SCALE + toep[i - j]
            kpos = j * BLK + lax.broadcasted_iota(jnp.int32, (BLK, BLK), 0)
            allowed = kpos >= first
            if i == j:
                allowed = allowed & (kpos <= qpos)
            sig = sigmoid(scores)
            act = scores * sig
            weights = jnp.where(allowed, act * (1.0 / SEQ), 0.0).astype(BF16)
            wts[p] = weights
            sgs[p] = jnp.where(allowed, (sig + act * (1.0 - sig)) * (1.0 / SEQ), 0.0)
            att = att + nn(actt[j, HD:2 * HD, :], weights)
        attt[i] = att

    def statistics(b):
        att = attt[b]
        up = dgr[b].astype(F32) * actt[b, 0:HD, :].astype(F32)
        mean = jnp.sum(att, axis=0, keepdims=True) * (1.0 / HD)
        cen = att - mean
        ats[2 * b] = cen[:, 0:ROWS].astype(BF16)
        ats[2 * b + 1] = cen[:, ROWS:].astype(BF16)
        rows = [
            mean,
            jnp.sum(cen * cen, axis=0, keepdims=True),
            jnp.sum(up, axis=0, keepdims=True),
            jnp.sum(up * cen, axis=0, keepdims=True),
        ]
        stat[b] = jnp.concatenate([q[:, :ROWS] for q in rows] + [q[:, ROWS:] for q in rows], axis=0)

    for b in (3, 2, 1, 0):
        forward(b)
    dg_sent.wait()
    for b in (3, 2, 1, 0):
        statistics(b)
    stats_sent = Copies(lambda t, landed: (
        stat, statr.at[from_ctx(t) if landed else ctx], sts.at[t], strr.at[t], (dp, ctx_peer(t))), 1, 8).start()
    statr[ctx] = stat[...]
    att_sent = all_to_all(ats, atr, gss, gsr).start()
    atr[ctx] = ats[ctx]

    def combined(b):
        parts = [
            jnp.concatenate([statr[r, b, 0:4], statr[r, b, 4:8]], axis=1) for r in range(HEADS)
        ]
        mean = sum([q[0:1] for q in parts]) * (1.0 / HEADS)
        var, s3, s4 = 0.0, 0.0, 0.0
        for q in parts:
            off = q[0:1] - mean
            var = var + q[1:2] + HD * off * off
            s3 = s3 + q[2:3]
            s4 = s4 + q[3:4] + off * q[2:3]
        inv = lax.rsqrt(var * (1.0 / D) + EPSILON)
        m1 = s3 * (1.0 / D)
        m2 = s4 * inv * (1.0 / D)
        norm = (attt[b] - mean) * inv
        dg = dgr[b].astype(F32)
        u = actt[b, 0:HD, :].astype(F32)
        dat[b] = ((dg * u - m1 - norm * m2) * inv).astype(BF16)
        uf[b] = dg * norm

    def backward(i):
        da = dat[i]
        dq = jnp.zeros((HD, BLK), F32)
        for j in range(i + 1):
            p = i * (i + 1) // 2 + j
            ds = (nn(vrow[j], da) * sgs[p]).astype(BF16)
            dq = dq + nn(actt[j, 3 * HD:, :], ds)
            dk = nt(actt[i, 2 * HD:3 * HD, :], ds)
            dv = nt(da, wts[p])
            if i < NBLK - 1:
                dk, dv = dk + dkt[j], dv + dvt[j]
            dkt[j] = dk
            dvt[j] = dv
        for part, val in enumerate((uf[i], dvt[i], dq * SCALE, dkt[i] * SCALE)):
            pre = pret[i, part * HD:(part + 1) * HD, :]
            sig = sigmoid(pre)
            dpt[i, part * HD:(part + 1) * HD, :] = (
                val * (sig * (1.0 + pre * (1.0 - sig)))
            ).astype(BF16)

    mates = {}

    def terms(b):
        theirs = pl.multiple_of((1 - core) * ROWS, ROWS)
        pd[b] = tn(dpt[b, :, pl.ds(theirs, ROWS)], wct[...]).astype(BF16)
        mates[b] = Copies(lambda t, landed: (pd.at[b], pdr.at[b], pds.at[b], pdsr.at[b], mate)).start()
        mine = pl.multiple_of(core * ROWS, ROWS)
        pm[b] = tn(dpt[b, :, pl.ds(mine, ROWS)], wct[...])

    half = (pl.ds(0, 64), pl.ds(64, 64))
    up = (dp, ((zh + 1) % 4) * 2 + core)
    down = (dp, ((zh + 3) % 4) * 2 + core)

    def round_copy(n, src, dst, to):
        return Copies(lambda t, landed: (src, dst, pss.at[n], psr.at[n], to))

    far = [
        round_copy(0, ps.at[2, half[0]], rr.at[0], up),
        round_copy(1, ps.at[2, half[1]], rr.at[1], down),
    ]
    near = {
        (1, 0): round_copy(2, ps.at[1, half[0]], pr.at[1, half[0]], up),
        (1, 1): round_copy(3, ps.at[1, half[1]], pr.at[1, half[1]], up),
        (3, 0): round_copy(4, ps.at[3, half[0]], pr.at[3, half[0]], down),
        (3, 1): round_copy(5, ps.at[3, half[1]], pr.at[3, half[1]], down),
    }
    started.extend(far)
    started.extend(near.values())

    def chip_sum(b):
        mates[b].wait()
        s = (b + 4 - zh) % 4

        @pl.when(s == 0)
        def _():
            own[...] = pm[b] + pdr[b].astype(F32)

        @pl.when(s == 2)
        def _():
            ps[2] = (pm[b] + pdr[b].astype(F32)).astype(BF16)
            far[0].go()
            far[1].go()

        @pl.when(s == 1)
        def _():
            ps[1, half[1]] = (pm[b, half[1]] + pdr[b, half[1]].astype(F32)).astype(BF16)
            near[1, 1].go()

        @pl.when(s == 3)
        def _():
            ps[3, half[0]] = (pm[b, half[0]] + pdr[b, half[0]].astype(F32)).astype(BF16)
            near[3, 0].go()

    def relay(b):
        s = (b + 4 - zh) % 4
        for n, way, h in ((0, 1, 0), (1, 3, 1)):
            @pl.when(s == way)
            def _():
                far[n].wait()
                ps[way, half[h]] = (
                    pm[b, half[h]] + pdr[b, half[h]].astype(F32) + rr[n].astype(F32)
                ).astype(BF16)
                near[way, h].go()

    stats_sent.wait()
    combined(3)
    backward(3)
    terms(3)

    u_sent.wait()
    att_sent.wait()
    mine = [jnp.where(core == 0, statr[r, zh, 0:4], statr[r, zh, 4:8]) for r in range(HEADS)]
    mean = sum([q[0:1] for q in mine]) * (1.0 / HEADS)
    var = 0.0
    for q in mine:
        off = q[0:1] - mean
        var = var + q[1:2] + HD * off * off
    inv = lax.rsqrt(var * (1.0 / D) + EPSILON)
    for r in range(HEADS):
        norm = (atr[r].astype(F32) + (mine[r][0:1] - mean)) * inv
        gto[r * HD:(r + 1) * HD] = (norm * utr[r].astype(F32)).astype(BF16)
    gated_mate = Copies(lambda t, landed: (gto, gtm, wds.at[1], wdr.at[1], mate)).start()
    combined(2)
    backward(2)
    chip_sum(3)
    terms(2)

    def ct_cols(which):
        return jnp.concatenate(
            [ctc[which, :, pl.ds(pl.multiple_of(b * BLK + core * HD, HD), HD)] for b in range(NBLK)], axis=1
        )

    gated_mate.wait()
    both = jnp.concatenate([gto[...], gtm[...]], axis=1)
    cts = jnp.concatenate([ct_cols(core), ct_cols(1 - core)], axis=0)
    wgs[...] = nn(both, cts).astype(BF16).reshape(2, PLANE, 32, 512)
    wg_plane = Copies(lambda t, landed: (
        wgs.at[:, plane_peer(t)], wgr.at[plane_from(t) if landed else yx], wgss.at[t], wgsr.at[t],
        (zl * PLANE + plane_peer(t), ctx)), 1, PLANE).start()
    wgr[yx] = wgs[:, yx]
    combined(1)
    backward(1)
    chip_sum(2)
    terms(1)
    combined(0)
    backward(0)
    chip_sum(1)
    terms(0)
    chip_sum(0)
    for b in (3, 2, 1, 0):
        relay(b)
    mates_half.wait()
    gated = gto[...]
    out_ref[...] = (
        xv[...].astype(F32)
        + tn(gated[0:512], wrb[0].reshape(512, D)) + tn(gated[512:], wrb[1].reshape(512, D))
    ).astype(BF16)

    wg_plane.wait()

    def add_plane(t, total):
        return total + wgr[t].astype(F32)

    wsum = lax.fori_loop(0, PLANE, add_plane, jnp.zeros((2, 32, 512), F32)).astype(BF16)
    for l in range(2):
        for h in range(4):
            wzs[l * 4 + h] = wsum[l, :, h * HD:(h + 1) * HD]

    zat = zl * 4 + zh

    def column(t, landed):
        to = (zat + t) % 8
        return (
            wzs.at[to], wzr.at[(zat + 8 - t) % 8 if landed else zat], wzss.at[t], wzsr.at[t],
            ((to // 4) * PLANE + yx, (to % 4) * 2 + core),
        )

    wg_column = Copies(column, 1, 8).start()
    wzr[zat] = wzs[zat]

    for c in near.values():
        c.wait()
    total = own[...] + pr[1].astype(F32) + pr[3].astype(F32)
    normed, inverse = normalize(xv[...].astype(F32))
    first = jnp.mean(total, axis=-1, keepdims=True)
    second = jnp.mean(total * normed, axis=-1, keepdims=True)
    grads_ref[...] = (
        ctc[core].astype(F32) + (total - first - normed * second) * inverse
    ).astype(BF16)

    wg_column.wait()
    wg_ref[...] = jnp.sum(wzr[...].astype(F32), axis=0)

    finish()


def on_device(inputs, input_weight, output_weight, cotangent, lengths, buckets, bias_weights):
    vm = lambda *shape, dt=BF16: pltpu.VMEM(shape, dt)
    sem = lambda n: pltpu.SemaphoreType.DMA((n,))
    scratch = [
        vm(8, ROWS, D), vm(2, 32, 512), vm(32, D), vm(32, D),
        vm(2, 4, 4, 32, 512), vm(2, 4, 4, 32, D),
        vm(512, D), vm(NBLK, 512, BLK, dt=F32), vm(NBLK, 512, BLK),
        vm(NBLK, BLK, HD), vm(NBLK, BLK, HD),
        vm(PAIRS, BLK, BLK), vm(PAIRS, BLK, BLK, dt=F32), vm(NBLK, BLK, BLK, dt=F32),
        vm(NBLK, HD, BLK, dt=F32), vm(NBLK, HD, BLK, dt=F32),
        vm(4, HD, BLK), vm(4, HD, BLK),
        vm(NBLK, 8, HD, dt=F32), vm(8, NBLK, 8, HD, dt=F32),
        vm(8, HD, ROWS), vm(8, HD, ROWS), vm(8, HD, ROWS), vm(8, HD, ROWS),
        vm(D, ROWS), vm(D, ROWS), vm(2, ROWS, D), vm(ROWS, D), vm(NBLK, HD, BLK),
        vm(NBLK, HD, BLK, dt=F32), vm(NBLK, HD, BLK, dt=F32),
        vm(NBLK, 512, BLK),
        vm(2, PLANE, 32, 512), vm(PLANE, 2, 32, 512),
        vm(8, 32, HD), vm(8, 32, HD),
        vm(NBLK, ROWS, D), vm(NBLK, ROWS, D), vm(NBLK, ROWS, D, dt=F32),
        vm(4, ROWS, D), vm(4, ROWS, D), vm(2, 64, D), vm(ROWS, D, dt=F32),
        sem(8), sem(8), sem(8), sem(8), sem(2), sem(2), sem(64), sem(64), sem(1), sem(1),
        sem(8), sem(8), sem(32), sem(32), sem(8), sem(8),
        sem(2), sem(2), sem(16), sem(16), sem(8), sem(8), sem(4), sem(4), sem(6), sem(6),
        sem(8), sem(8), sem(7),
    ]
    vspec = pl.BlockSpec(memory_space=pltpu.VMEM)
    aspec = pl.BlockSpec(memory_space=pl.ANY)
    sspec = pl.BlockSpec(memory_space=pltpu.SMEM)
    return pl.pallas_call(
        kernel,
        name="hstu",
        out_shape=(
            jax.ShapeDtypeStruct((ROWS, D), BF16),
            jax.ShapeDtypeStruct((ROWS, D), BF16),
            jax.ShapeDtypeStruct((32, HD), F32),
        ),
        in_specs=[sspec, sspec, vspec, aspec, aspec, aspec, aspec],
        out_specs=(vspec, vspec, vspec),
        scratch_shapes=scratch,
        compiler_params=pltpu.CompilerParams(
            collective_id=0, has_side_effects=True, vmem_limit_bytes=56 << 20
        ),
    )(lengths, bias_weights, buckets.reshape(1, SEQ), inputs, input_weight, output_weight, cotangent)


def solution(mesh):
    return jax.shard_map(
        on_device,
        mesh=mesh,
        in_specs=(
            P(("dp", "ctx"), None),
            P("dp", None),
            P("dp", None),
            P(("dp", "ctx"), None),
            P("dp", None),
            P(),
            P(),
        ),
        out_specs=(P(("dp", "ctx"), None), P(("dp", "ctx"), None), P("dp", "ctx")),
        check_vma=False,
    )
```

```python
import functools
import math

import jax
import jax.numpy as jnp
from jax import lax
from jax.experimental import pallas as pl
from jax.experimental.pallas import tpu as pltpu
from jax.sharding import PartitionSpec as P

EPSILON = 1e-06
MESH = pl.DeviceIdType.MESH
F32 = jnp.float32
BF16 = jnp.bfloat16

ROWS = 128
BLK = 256
NBLK = 4
HEADS = 8
HD = 128
D = 1024
SEQ = 1024
PLANE = 16
PAIRS = NBLK * (NBLK + 1) // 2
SCALE = 1.0 / math.sqrt(HD)


def nn(a, b):
    return lax.dot_general(a, b, (((1,), (0,)), ((), ())), preferred_element_type=F32)


def nt(a, b):
    return lax.dot_general(a, b, (((1,), (1,)), ((), ())), preferred_element_type=F32)


def tn(a, b):
    return lax.dot_general(a, b, (((0,), (0,)), ((), ())), preferred_element_type=F32)


def sigmoid(values):
    return 0.5 * jnp.tanh(0.5 * values) + 0.5


def normalize(values):
    average = jnp.mean(values, axis=-1, keepdims=True)
    centered = values - average
    inverse = lax.rsqrt(jnp.mean(centered * centered, axis=-1, keepdims=True) + EPSILON)
    return (centered * inverse, inverse)


def kernel(
    lengths_ref, bias_ref, buckets_ref, x_ref, win_ref, wout_ref, ct_ref,
    out_ref, grads_ref, wg_ref,
    xg, wa, wb, wbo, wra, wrb, wct, pret, actt, krow, vrow, wts, sgs, toep, attt, uf,
    dgs, dgr, stat, statr, gstat, gstatr, moments, gts, gtr, gtm, ctc, xv, dat, dkt, dvt, dpt,
    wgs, wgr, wzs, wzr,
    pd, pdr, pm, ps, pr, rr, own,
    xs, xr, xfs, xfr, was, war, wps, wpr, wos, wor, dss, dsr, sts, strr, gss, gsr,
    wds, wdr, wgss, wgsr, wzss, wzsr, pds, pdsr, pss, psr, lds,
):
    dp = lax.axis_index("dp")
    ctx = lax.axis_index("ctx")
    zh, core = ctx // 2, ctx % 2
    zl, yx = dp // PLANE, dp % PLANE
    y, x = yx // 4, yx % 4
    mate = (dp, zh * 2 + 1 - core)

    def ctx_peer(t):
        return (ctx + t) % 8

    def plane_peer(t):
        return ((y + t // 4) % 4) * 4 + (x + t % 4) % 4

    def plane_from(t):
        return ((y + 4 - t // 4) % 4) * 4 + (x + 4 - t % 4) % 4

    started = []

    class Copies:
        def __init__(self, make, lo=0, hi=1, where=None):
            self.make, self.lo, self.hi, self.where, self.received = make, lo, hi, where, False

        def each(self, act, landed=False):
            def one(t, _):
                if self.where is None:
                    run(t)
                else:
                    pl.when(self.where(t, landed))(lambda: run(t))
                return 0

            def run(t):
                src, dst, ss, rs, dev = self.make(t, landed)
                act(
                    pltpu.make_async_remote_copy(
                        src_ref=src, dst_ref=dst, send_sem=ss, recv_sem=rs,
                        device_id=dev, device_id_type=MESH,
                    )
                )

            if self.hi - self.lo == 1:
                one(self.lo, 0)
            else:
                lax.fori_loop(self.lo, self.hi, one, 0)

        def go(self):
            self.each(lambda c: c.start())

        def start(self):
            started.append(self)
            self.go()
            return self

        def wait(self):
            self.received = True
            self.each(lambda c: c.wait_recv(), True)

        def sent(self):
            self.each(lambda c: c.wait_send())

    def finish():
        for c in started:
            if not c.received:
                c.wait()
        for c in started:
            c.sent()

    barrier = pltpu.get_barrier_semaphore()

    def greet_ctx(t, _):
        pl.semaphore_signal(barrier, inc=1, device_id=(dp, ctx_peer(t)), device_id_type=MESH)
        return 0

    def greet_plane(t, _):
        pl.semaphore_signal(
            barrier, inc=1, device_id=(zl * PLANE + plane_peer(t), ctx), device_id_type=MESH
        )
        return 0

    def greet_column(t, _):
        pl.semaphore_signal(
            barrier, inc=1, device_id=((1 - zl) * PLANE + yx, t * 2 + core), device_id_type=MESH
        )
        return 0

    lax.fori_loop(1, 8, greet_ctx, 0)
    lax.fori_loop(1, 16, greet_plane, 0)
    lax.fori_loop(0, 4, greet_column, 0)

    load_x = pltpu.make_async_copy(x_ref, xv, lds.at[0])
    load_x.start()
    load_w = [
        pltpu.make_async_copy(wout_ref, wbo, lds.at[1])
    ]
    for part in range(4):
        at = pl.multiple_of(part * D + ctx * HD, HD)
        load_w.append(
            pltpu.make_async_copy(
                win_ref.at[:, pl.ds(at, HD)], wa.at[zl, :, pl.ds(part * HD, HD)], lds.at[2 + part]
            )
        )
    for c in load_w:
        c.start()
    load_ct = pltpu.make_async_copy(ct_ref, ctc.at[core], lds.at[6])
    load_ct.start()
    load_x.wait()
    normed, _ = normalize(xv[...].astype(F32))
    xg[ctx] = normed.astype(BF16)
    for c in load_w:
        c.wait()

    pl.semaphore_wait(barrier, 26)

    other = ((1 - zl) * PLANE + yx, ctx)

    def across(ref, k):
        return Copies(lambda t, landed: (
            ref.at[zl], ref.at[1 - zl if landed else zl], was.at[k], war.at[k], other))

    def half_rows(r, h):
        return xg.at[r, pl.ds(h * 64, 64)]

    def own_rows(s, h):
        src = ((zh + 4 - s) % 4) * 2 + core
        return Copies(lambda t, landed: (
            half_rows(ctx, h), half_rows(src if landed else ctx, h), xs.at[s * 2 + h], xr.at[s * 2 + h],
            (dp, ((zh + s) % 4) * 2 + core)))

    def relayed_rows(s, h):
        src = ((zh + 4 - s) % 4) * 2 + core
        far = ((zh + 2) % 4) * 2 + core
        return Copies(lambda t, landed: (
            half_rows(src, h), half_rows(far if landed else src, h), xs.at[4 + h], xr.at[4 + h],
            (dp, ((zh + s) % 4) * 2 + core)))

    def mate_rows(s, h):
        chip = ((zh + 4 - s) % 4) * 2
        return Copies(lambda t, landed: (
            half_rows(chip + core, h), half_rows(chip + (1 - core if landed else core), h),
            xfs.at[s * 2 + h], xfr.at[s * 2 + h], mate))

    def step_by(axis, ty, tx, t):
        return (ty, (tx + t) % 4) if axis == "x" else ((ty + t) % 4, tx)

    def in_plane(place):
        return (zl * PLANE + place[0] * 4 + place[1], ctx)

    class Spread:
        def __init__(self, src, dst, axis, base):
            self.src, self.dst, self.axis, self.base = src, dst, axis, base
            self.cross = "y" if axis == "x" else "x"
            self.first, self.rest = [], []

        def own(self):
            for axis in (self.axis, self.cross):
                for t in (1, 3, 2):
                    at = self.base + (axis == self.cross) * 3 + t - 1

                    def make(_, landed, axis=axis, t=t, at=at):
                        py, px = step_by(axis, y, x, 4 - t) if landed else (y, x)
                        return (self.src, self.dst(py, px), wps.at[at], wpr.at[at],
                                in_plane(step_by(axis, y, x, t)))

                    (self.first if axis == self.axis else self.rest).append(Copies(make).start())

        def hand_on(self):
            for n, t in enumerate((1, 3, 2)):
                self.first[n].wait()
                for u in (1, 3, 2):
                    at = self.base + 6 + (t - 1) * 3 + u - 1

                    def make(_, landed, t=t, u=u, at=at):
                        py, px = step_by(self.axis, y, x, 4 - t)
                        ty, tx = step_by(self.cross, py, px, 4 - u) if landed else (py, px)
                        return (self.dst(py, px), self.dst(ty, tx), wps.at[at], wpr.at[at],
                                in_plane(step_by(self.cross, y, x, u)))

                    self.rest.append(Copies(make).start())

        def wait(self):
            for c in self.rest:
                c.wait()

    def from_ctx(t):
        return (ctx + 8 - t) % 8

    def all_to_all(src, dst, ss, rs):
        return Copies(lambda t, landed: (
            src.at[ctx_peer(t)], dst.at[from_ctx(t) if landed else ctx], ss.at[t], rs.at[t],
            (dp, ctx_peer(t))), 1, 8)

    mine_b = zl == core
    xb = Copies(lambda t, landed: (wbo, wb, was.at[1], war.at[1], other), where=lambda t, landed: (
        jnp.logical_not(mine_b) if landed else mine_b)).start()
    xa = across(wa, 0).start()
    to_mate_rows = [[None, None] for _ in range(4)]
    for h in range(2):
        to_mate_rows[0][h] = mate_rows(0, h).start()
    up0, down1 = own_rows(1, 0).start(), own_rows(3, 1).start()
    up1, down0 = own_rows(1, 1).start(), own_rows(3, 0).start()
    @pl.when(mine_b)
    def _():
        wb[...] = wbo[...]

    xb.wait()
    lo, hi = pl.ds(0, 512), pl.ds(512, 512)
    out_spread = [
        Spread(wb.at[:, lo], lambda py, px: wrb.at[core, py, px, :, lo], "x", 0),
        Spread(wb.at[:, hi], lambda py, px: wrb.at[core, py, px, :, hi], "y", 16),
    ]
    for w in out_spread:
        w.own()
    load_ct.wait()
    ct_mate = Copies(lambda t, landed: (
        ctc.at[core], ctc.at[1 - core if landed else core], wds.at[0], wdr.at[0], mate)).start()
    xa.wait()
    low, high = pl.ds(0, 256), pl.ds(256, 256)
    in_spread = [
        Spread(wa.at[:, :, low], lambda py, px: wra.at[:, py, px, :, low], "x", 32),
        Spread(wa.at[:, :, high], lambda py, px: wra.at[:, py, px, :, high], "y", 48),
    ]
    for w in in_spread:
        w.own()
    wrb[core, y, x] = wb[...]
    wra[:, y, x] = wa[...]
    for w in out_spread:
        w.hand_on()

    buckets = buckets_ref[...]
    table = jnp.zeros((1, SEQ), F32)
    for b in range(32):
        table = jnp.where(buckets == b, bias_ref[ctx, b], table)
    padded = jnp.concatenate([table[:, 0:BLK], table], axis=1)
    for d in range(NBLK):
        wide = jnp.broadcast_to(padded[:, d * BLK:d * BLK + 2 * BLK], (BLK, 2 * BLK))
        toep[d] = pltpu.roll(wide, 0, 1, stride=1, stride_axis=0)[:, BLK:]

    up0.wait()
    far0 = relayed_rows(1, 0).start()
    to_mate_rows[1][0] = mate_rows(1, 0).start()
    down1.wait()
    far1 = relayed_rows(3, 1).start()
    to_mate_rows[3][1] = mate_rows(3, 1).start()
    up1.wait()
    to_mate_rows[1][1] = mate_rows(1, 1).start()
    down0.wait()
    to_mate_rows[3][0] = mate_rows(3, 0).start()

    for w in in_spread:
        w.hand_on()

    for w in out_spread:
        w.wait()
    ct_mate.wait()
    ct_chip = ctc[...].reshape(BLK, D)
    wout_half = wrb[core].reshape(512, D)
    for n in range(4):
        dgs[n] = nt(wout_half[n * HD:(n + 1) * HD], ct_chip).astype(BF16)

    def head_at(n):
        return core * 4 + n

    from_half = zh // 2
    dg_sent = Copies(
        lambda t, landed: (
            dgs.at[t], dgr.at[t if landed else zh], dss.at[t], dsr.at[t if landed else zh], (dp, head_at(t))),
        0, 4,
        where=lambda t, landed: (t * 2 + from_half != ctx) if landed else (head_at(t) != ctx),
    ).start()

    @pl.when(from_half == core)
    def _():
        dgr[zh] = dgs[ctx % 4]

    mates_half = Copies(lambda t, landed: (
        wrb.at[core], wrb.at[1 - core if landed else core], wos.at[0], wor.at[0], mate)).start()

    for w in in_spread:
        w.wait()
    for part in range(4):
        piece = wra[:, :, :, :, part * HD:(part + 1) * HD].reshape(D, HD)
        wct[part * HD:(part + 1) * HD, :] = piece.T

    def project(zb):
        rows = xg[pl.ds(zb * 2, 2)].reshape(BLK, D)
        pre = nt(wct[...], rows)
        pret[zb] = pre
        acts = (pre * sigmoid(pre)).astype(BF16)
        actt[zb] = acts
        vrow[zb] = acts[HD:2 * HD].T
        krow[zb] = acts[3 * HD:].T

    for s in (0, 1, 3):
        for h in range(2):
            to_mate_rows[s][h].wait()
        project((zh + 4 - s) % 4)
    far0.wait()
    to_mate_rows[2][0] = mate_rows(2, 0).start()
    far1.wait()
    to_mate_rows[2][1] = mate_rows(2, 1).start()
    for h in range(2):
        to_mate_rows[2][h].wait()
    project((zh + 2) % 4)

    l0, l1, l2 = lengths_ref[0, 0], lengths_ref[0, 1], lengths_ref[0, 2]
    e0, e1, e2 = l0, l0 + l1, l0 + l1 + l2

    def forward(i):
        qpos = i * BLK + lax.broadcasted_iota(jnp.int32, (1, BLK), 1)
        first = jnp.where(qpos >= e2, e2, jnp.where(qpos >= e1, e1, jnp.where(qpos >= e0, e0, 0)))
        att = jnp.zeros((HD, BLK), F32)
        for j in range(i + 1):
            p = i * (i + 1) // 2 + j
            scores = nn(krow[j], actt[i, 2 * HD:3 * HD, :]) * SCALE + toep[i - j]
            kpos = j * BLK + lax.broadcasted_iota(jnp.int32, (BLK, BLK), 0)
            allowed = kpos >= first
            if i == j:
                allowed = allowed & (kpos <= qpos)
            sig = sigmoid(scores)
            act = scores * sig
            weights = jnp.where(allowed, act * (1.0 / SEQ), 0.0).astype(BF16)
            wts[p] = weights
            sgs[p] = jnp.where(allowed, (sig + act * (1.0 - sig)) * (1.0 / SEQ), 0.0)
            att = att + nn(actt[j, HD:2 * HD, :], weights)
        attt[i] = att

    def packed(ref, pieces):
        for n in range(2):
            rows = []
            for b in (2 * n, 2 * n + 1):
                rows += [q[:, :ROWS] for q in pieces[b]] + [q[:, ROWS:] for q in pieces[b]]
            ref[n] = jnp.concatenate(rows, axis=0)

    def unpacked(ref, r, b):
        q = ref[r, b // 2, (b % 2) * 4:(b % 2) * 4 + 4]
        return (
            jnp.concatenate([q[0:1], q[2:3]], axis=1), jnp.concatenate([q[1:2], q[3:4]], axis=1)
        )

    def to_group(src, dst, base):
        return Copies(lambda t, landed: (
            src, dst.at[from_ctx(t) if landed else ctx], sts.at[base + t], strr.at[base + t],
            (dp, ctx_peer(t))), 1, 8).start()

    for b in (3, 2, 1, 0):
        forward(b)
    pieces = []
    for b in range(NBLK):
        att = attt[b]
        mean = jnp.sum(att, axis=0, keepdims=True) * (1.0 / HD)
        cen = att - mean
        pieces.append((mean, jnp.sum(cen * cen, axis=0, keepdims=True)))
    packed(stat, pieces)
    att_stats = to_group(stat, statr, 0)
    statr[ctx] = stat[...]

    dg_sent.wait()
    grads = []
    for b in range(NBLK):
        cen = attt[b] - pieces[b][0]
        up = dgr[b].astype(F32) * actt[b, 0:HD, :].astype(F32)
        grads.append((jnp.sum(up, axis=0, keepdims=True), jnp.sum(up * cen, axis=0, keepdims=True)))
    packed(gstat, grads)
    grad_stats = to_group(gstat, gstatr, 8)
    gstatr[ctx] = gstat[...]

    att_stats.wait()
    for b in range(NBLK):
        heads = [unpacked(statr, r, b) for r in range(HEADS)]
        mean = sum([m for m, _ in heads]) * (1.0 / HEADS)
        var = 0.0
        for m, v in heads:
            var = var + v + HD * (m - mean) * (m - mean)
        inv = lax.rsqrt(var * (1.0 / D) + EPSILON)
        norm = (attt[b] - mean) * inv
        attt[b] = norm
        moments[b, 0:1] = mean
        moments[b, 1:2] = inv
        gated = (norm * actt[b, 0:HD, :].astype(F32)).astype(BF16)
        gts[2 * b] = gated[:, 0:ROWS]
        gts[2 * b + 1] = gated[:, ROWS:]
    gated_sent = all_to_all(gts, gtr, gss, gsr).start()
    gtr[ctx] = gts[ctx]

    def combined(b):
        mean, inv = moments[b, 0:1], moments[b, 1:2]
        s3, s4 = 0.0, 0.0
        for r in range(HEADS):
            p, q = unpacked(gstatr, r, b)
            s3 = s3 + p
            s4 = s4 + q + (unpacked(statr, r, b)[0] - mean) * p
        m1 = s3 * (1.0 / D)
        m2 = s4 * inv * (1.0 / D)
        norm = attt[b]
        dg = dgr[b].astype(F32)
        u = actt[b, 0:HD, :].astype(F32)
        dat[b] = ((dg * u - m1 - norm * m2) * inv).astype(BF16)
        uf[b] = dg * norm

    def backward(i):
        da = dat[i]
        dq = jnp.zeros((HD, BLK), F32)
        for j in range(i + 1):
            p = i * (i + 1) // 2 + j
            ds = (nn(vrow[j], da) * sgs[p]).astype(BF16)
            dq = dq + nn(actt[j, 3 * HD:, :], ds)
            dk = nt(actt[i, 2 * HD:3 * HD, :], ds)
            dv = nt(da, wts[p])
            if i < NBLK - 1:
                dk, dv = dk + dkt[j], dv + dvt[j]
            dkt[j] = dk
            dvt[j] = dv
        for part, val in enumerate((uf[i], dvt[i], dq * SCALE, dkt[i] * SCALE)):
            pre = pret[i, part * HD:(part + 1) * HD, :]
            sig = sigmoid(pre)
            dpt[i, part * HD:(part + 1) * HD, :] = (
                val * (sig * (1.0 + pre * (1.0 - sig)))
            ).astype(BF16)

    mates = {}

    def terms(b):
        theirs = pl.multiple_of((1 - core) * ROWS, ROWS)
        pd[b] = tn(dpt[b, :, pl.ds(theirs, ROWS)], wct[...]).astype(BF16)
        mates[b] = Copies(lambda t, landed: (pd.at[b], pdr.at[b], pds.at[b], pdsr.at[b], mate)).start()
        mine = pl.multiple_of(core * ROWS, ROWS)
        pm[b] = tn(dpt[b, :, pl.ds(mine, ROWS)], wct[...])

    half = (pl.ds(0, 64), pl.ds(64, 64))
    up = (dp, ((zh + 1) % 4) * 2 + core)
    down = (dp, ((zh + 3) % 4) * 2 + core)

    def round_copy(n, src, dst, to):
        return Copies(lambda t, landed: (src, dst, pss.at[n], psr.at[n], to))

    far = [
        round_copy(0, ps.at[2, half[0]], rr.at[0], up),
        round_copy(1, ps.at[2, half[1]], rr.at[1], down),
    ]
    near = {
        (1, 0): round_copy(2, ps.at[1, half[0]], pr.at[1, half[0]], up),
        (1, 1): round_copy(3, ps.at[1, half[1]], pr.at[1, half[1]], up),
        (3, 0): round_copy(4, ps.at[3, half[0]], pr.at[3, half[0]], down),
        (3, 1): round_copy(5, ps.at[3, half[1]], pr.at[3, half[1]], down),
    }
    started.extend(far)
    started.extend(near.values())

    def chip_sum(b):
        mates[b].wait()
        s = (b + 4 - zh) % 4

        @pl.when(s == 0)
        def _():
            own[...] = pm[b] + pdr[b].astype(F32)

        @pl.when(s == 2)
        def _():
            ps[2] = (pm[b] + pdr[b].astype(F32)).astype(BF16)
            far[0].go()
            far[1].go()

        @pl.when(s == 1)
        def _():
            ps[1, half[1]] = (pm[b, half[1]] + pdr[b, half[1]].astype(F32)).astype(BF16)
            near[1, 1].go()

        @pl.when(s == 3)
        def _():
            ps[3, half[0]] = (pm[b, half[0]] + pdr[b, half[0]].astype(F32)).astype(BF16)
            near[3, 0].go()

    def relay(b):
        s = (b + 4 - zh) % 4
        for n, way, h in ((0, 1, 0), (1, 3, 1)):
            @pl.when(s == way)
            def _():
                far[n].wait()
                ps[way, half[h]] = (
                    pm[b, half[h]] + pdr[b, half[h]].astype(F32) + rr[n].astype(F32)
                ).astype(BF16)
                near[way, h].go()

    def ct_cols(which):
        return jnp.concatenate(
            [ctc[which, :, pl.ds(pl.multiple_of(b * BLK + core * HD, HD), HD)] for b in range(NBLK)], axis=1
        )

    grad_stats.wait()
    combined(3)
    backward(3)
    terms(3)
    combined(2)
    backward(2)
    chip_sum(3)
    terms(2)

    gated_sent.wait()
    gated_mate = Copies(lambda t, landed: (gtr, gtm, wds.at[1], wdr.at[1], mate)).start()
    combined(1)
    backward(1)
    chip_sum(2)
    terms(1)
    gated_mate.wait()
    both = jnp.concatenate([gtr[...].reshape(D, ROWS), gtm[...].reshape(D, ROWS)], axis=1)
    cts = jnp.concatenate([ct_cols(core), ct_cols(1 - core)], axis=0)
    wgs[...] = nn(both, cts).astype(BF16).reshape(2, PLANE, 32, 512)
    wg_plane = Copies(lambda t, landed: (
        wgs.at[:, plane_peer(t)], wgr.at[plane_from(t) if landed else yx], wgss.at[t], wgsr.at[t],
        (zl * PLANE + plane_peer(t), ctx)), 1, PLANE).start()
    wgr[yx] = wgs[:, yx]
    combined(0)
    backward(0)
    chip_sum(1)
    terms(0)
    chip_sum(0)
    for b in (3, 2, 1, 0):
        relay(b)
    mates_half.wait()
    gated = gtr[...].reshape(D, ROWS)
    out_ref[...] = (
        xv[...].astype(F32)
        + tn(gated[0:512], wrb[0].reshape(512, D)) + tn(gated[512:], wrb[1].reshape(512, D))
    ).astype(BF16)

    wg_plane.wait()

    def add_plane(t, total):
        return total + wgr[t].astype(F32)

    wsum = lax.fori_loop(0, PLANE, add_plane, jnp.zeros((2, 32, 512), F32)).astype(BF16)
    for l in range(2):
        for h in range(4):
            wzs[l * 4 + h] = wsum[l, :, h * HD:(h + 1) * HD]

    zat = zl * 4 + zh

    def column(t, landed):
        to = (zat + t) % 8
        return (
            wzs.at[to], wzr.at[(zat + 8 - t) % 8 if landed else zat], wzss.at[t], wzsr.at[t],
            ((to // 4) * PLANE + yx, (to % 4) * 2 + core),
        )

    wg_column = Copies(column, 1, 8).start()
    wzr[zat] = wzs[zat]

    for c in near.values():
        c.wait()
    total = own[...] + pr[1].astype(F32) + pr[3].astype(F32)
    normed, inverse = normalize(xv[...].astype(F32))
    first = jnp.mean(total, axis=-1, keepdims=True)
    second = jnp.mean(total * normed, axis=-1, keepdims=True)
    grads_ref[...] = (
        ctc[core].astype(F32) + (total - first - normed * second) * inverse
    ).astype(BF16)

    wg_column.wait()
    wg_ref[...] = jnp.sum(wzr[...].astype(F32), axis=0)

    finish()


def on_device(inputs, input_weight, output_weight, cotangent, lengths, buckets, bias_weights):
    vm = lambda *shape, dt=BF16: pltpu.VMEM(shape, dt)
    sem = lambda n: pltpu.SemaphoreType.DMA((n,))
    scratch = [
        vm(8, ROWS, D), vm(2, 32, 512), vm(32, D), vm(32, D),
        vm(2, 4, 4, 32, 512), vm(2, 4, 4, 32, D),
        vm(512, D), vm(NBLK, 512, BLK, dt=F32), vm(NBLK, 512, BLK),
        vm(NBLK, BLK, HD), vm(NBLK, BLK, HD),
        vm(PAIRS, BLK, BLK), vm(PAIRS, BLK, BLK, dt=F32), vm(NBLK, BLK, BLK, dt=F32),
        vm(NBLK, HD, BLK, dt=F32), vm(NBLK, HD, BLK, dt=F32),
        vm(4, HD, BLK), vm(4, HD, BLK),
        vm(2, 8, HD, dt=F32), vm(8, 2, 8, HD, dt=F32), vm(2, 8, HD, dt=F32), vm(8, 2, 8, HD, dt=F32),
        vm(NBLK, 8, BLK, dt=F32),
        vm(8, HD, ROWS), vm(8, HD, ROWS), vm(8, HD, ROWS), vm(2, ROWS, D), vm(ROWS, D), vm(NBLK, HD, BLK),
        vm(NBLK, HD, BLK, dt=F32), vm(NBLK, HD, BLK, dt=F32),
        vm(NBLK, 512, BLK),
        vm(2, PLANE, 32, 512), vm(PLANE, 2, 32, 512),
        vm(8, 32, HD), vm(8, 32, HD),
        vm(NBLK, ROWS, D), vm(NBLK, ROWS, D), vm(NBLK, ROWS, D, dt=F32),
        vm(4, ROWS, D), vm(4, ROWS, D), vm(2, 64, D), vm(ROWS, D, dt=F32),
        sem(8), sem(8), sem(8), sem(8), sem(2), sem(2), sem(64), sem(64), sem(1), sem(1),
        sem(8), sem(8), sem(32), sem(32), sem(8), sem(8),
        sem(2), sem(2), sem(16), sem(16), sem(8), sem(8), sem(4), sem(4), sem(6), sem(6),
        sem(7),
    ]
    vspec = pl.BlockSpec(memory_space=pltpu.VMEM)
    aspec = pl.BlockSpec(memory_space=pl.ANY)
    sspec = pl.BlockSpec(memory_space=pltpu.SMEM)
    return pl.pallas_call(
        kernel,
        name="hstu",
        out_shape=(
            jax.ShapeDtypeStruct((ROWS, D), BF16),
            jax.ShapeDtypeStruct((ROWS, D), BF16),
            jax.ShapeDtypeStruct((32, HD), F32),
        ),
        in_specs=[sspec, sspec, vspec, aspec, aspec, aspec, aspec],
        out_specs=(vspec, vspec, vspec),
        scratch_shapes=scratch,
        compiler_params=pltpu.CompilerParams(
            collective_id=0, has_side_effects=True, vmem_limit_bytes=56 << 20
        ),
    )(lengths, bias_weights, buckets.reshape(1, SEQ), inputs, input_weight, output_weight, cotangent)


def solution(mesh):
    return jax.shard_map(
        on_device,
        mesh=mesh,
        in_specs=(
            P(("dp", "ctx"), None),
            P("dp", None),
            P("dp", None),
            P(("dp", "ctx"), None),
            P("dp", None),
            P(),
            P(),
        ),
        out_specs=(P(("dp", "ctx"), None), P(("dp", "ctx"), None), P("dp", "ctx")),
        check_vma=False,
    )
```

```python
import functools
import math

import jax
import jax.numpy as jnp
from jax import lax
from jax.experimental import pallas as pl
from jax.experimental.pallas import tpu as pltpu
from jax.sharding import PartitionSpec as P

EPSILON = 1e-06
MESH = pl.DeviceIdType.MESH
F32 = jnp.float32
BF16 = jnp.bfloat16

ROWS = 128
BLK = 256
NBLK = 4
HEADS = 8
HD = 128
D = 1024
SEQ = 1024
PLANE = 16
PAIRS = NBLK * (NBLK + 1) // 2
SCALE = 1.0 / math.sqrt(HD)


def nn(a, b):
    return lax.dot_general(a, b, (((1,), (0,)), ((), ())), preferred_element_type=F32)


def nt(a, b):
    return lax.dot_general(a, b, (((1,), (1,)), ((), ())), preferred_element_type=F32)


def tn(a, b):
    return lax.dot_general(a, b, (((0,), (0,)), ((), ())), preferred_element_type=F32)


def sigmoid(values):
    return 0.5 * jnp.tanh(0.5 * values) + 0.5


def normalize(values):
    average = jnp.mean(values, axis=-1, keepdims=True)
    centered = values - average
    inverse = lax.rsqrt(jnp.mean(centered * centered, axis=-1, keepdims=True) + EPSILON)
    return (centered * inverse, inverse)


def kernel(
    lengths_ref, bias_ref, buckets_ref, x_ref, win_ref, wout_ref, ct_ref,
    out_ref, grads_ref, wg_ref,
    xg, wa, wb, wbo, wra, wrb, wct, pret, actt, krow, vrow, wts, sgs, toep, attt, uf,
    dgs, dgr, stat, statr, gstat, gstatr, moments, gts, gtr, gtm, ctc, xv, dat, dkt, dvt, dpt,
    wgs, wgr, wzs, wzr,
    pd, pdr, pm, ps, pr, rr, own,
    xs, xr, xfs, xfr, was, war, wps, wpr, wos, wor, dss, dsr, sts, strr, gss, gsr,
    wds, wdr, wgss, wgsr, wzss, wzsr, pds, pdsr, pss, psr, lds,
):
    dp = lax.axis_index("dp")
    ctx = lax.axis_index("ctx")
    zh, core = ctx // 2, ctx % 2
    zl, yx = dp // PLANE, dp % PLANE
    y, x = yx // 4, yx % 4
    mate = (dp, zh * 2 + 1 - core)

    def ctx_peer(t):
        return (ctx + t) % 8

    def plane_peer(t):
        return ((y + t // 4) % 4) * 4 + (x + t % 4) % 4

    def plane_from(t):
        return ((y + 4 - t // 4) % 4) * 4 + (x + 4 - t % 4) % 4

    started = []

    class Copies:
        def __init__(self, make, lo=0, hi=1, where=None):
            self.make, self.lo, self.hi, self.where, self.received = make, lo, hi, where, False

        def each(self, act, landed=False):
            def one(t, _):
                if self.where is None:
                    run(t)
                else:
                    pl.when(self.where(t, landed))(lambda: run(t))
                return 0

            def run(t):
                src, dst, ss, rs, dev = self.make(t, landed)
                act(
                    pltpu.make_async_remote_copy(
                        src_ref=src, dst_ref=dst, send_sem=ss, recv_sem=rs,
                        device_id=dev, device_id_type=MESH,
                    )
                )

            if self.hi - self.lo == 1:
                one(self.lo, 0)
            else:
                lax.fori_loop(self.lo, self.hi, one, 0)

        def go(self):
            self.each(lambda c: c.start())

        def start(self):
            started.append(self)
            self.go()
            return self

        def wait(self):
            self.received = True
            self.each(lambda c: c.wait_recv(), True)

        def sent(self):
            self.each(lambda c: c.wait_send())

    def settle(later=()):
        for c in [c for c in started if c not in later]:
            c.sent()
            started.remove(c)

    def finish():
        for c in started:
            if not c.received:
                c.wait()
        settle()

    barrier = pltpu.get_barrier_semaphore()

    def greet_ctx(t, _):
        pl.semaphore_signal(barrier, inc=1, device_id=(dp, ctx_peer(t)), device_id_type=MESH)
        return 0

    def greet_plane(t, _):
        pl.semaphore_signal(
            barrier, inc=1, device_id=(zl * PLANE + plane_peer(t), ctx), device_id_type=MESH
        )
        return 0

    def greet_column(t, _):
        pl.semaphore_signal(
            barrier, inc=1, device_id=((1 - zl) * PLANE + yx, t * 2 + core), device_id_type=MESH
        )
        return 0

    lax.fori_loop(1, 8, greet_ctx, 0)
    lax.fori_loop(1, 16, greet_plane, 0)
    lax.fori_loop(0, 4, greet_column, 0)

    load_x = pltpu.make_async_copy(x_ref, xv, lds.at[0])
    load_x.start()
    load_w = [
        pltpu.make_async_copy(wout_ref, wbo, lds.at[1])
    ]
    for part in range(4):
        at = pl.multiple_of(part * D + ctx * HD, HD)
        load_w.append(
            pltpu.make_async_copy(
                win_ref.at[:, pl.ds(at, HD)], wa.at[zl, :, pl.ds(part * HD, HD)], lds.at[2 + part]
            )
        )
    for c in load_w:
        c.start()
    load_ct = pltpu.make_async_copy(ct_ref, ctc.at[core], lds.at[6])
    load_ct.start()
    load_x.wait()
    normed, _ = normalize(xv[...].astype(F32))
    xg[ctx] = normed.astype(BF16)
    for c in load_w:
        c.wait()

    buckets = buckets_ref[...]
    table = jnp.zeros((1, SEQ), F32)
    for b in range(32):
        table = jnp.where(buckets == b, bias_ref[ctx, b], table)
    padded = jnp.concatenate([table[:, 0:BLK], table], axis=1)
    for d in range(NBLK):
        wide = jnp.broadcast_to(padded[:, d * BLK:d * BLK + 2 * BLK], (BLK, 2 * BLK))
        toep[d] = pltpu.roll(wide, 0, 1, stride=1, stride_axis=0)[:, BLK:]

    pl.semaphore_wait(barrier, 26)

    other = ((1 - zl) * PLANE + yx, ctx)

    def across(ref, k):
        return Copies(lambda t, landed: (
            ref.at[zl], ref.at[1 - zl if landed else zl], was.at[k], war.at[k], other))

    def half_rows(r, h):
        return xg.at[r, pl.ds(h * 64, 64)]

    def own_rows(s, h):
        src = ((zh + 4 - s) % 4) * 2 + core
        return Copies(lambda t, landed: (
            half_rows(ctx, h), half_rows(src if landed else ctx, h), xs.at[s * 2 + h], xr.at[s * 2 + h],
            (dp, ((zh + s) % 4) * 2 + core)))

    def relayed_rows(s, h):
        src = ((zh + 4 - s) % 4) * 2 + core
        far = ((zh + 2) % 4) * 2 + core
        return Copies(lambda t, landed: (
            half_rows(src, h), half_rows(far if landed else src, h), xs.at[4 + h], xr.at[4 + h],
            (dp, ((zh + s) % 4) * 2 + core)))

    def mate_rows(s, h):
        chip = ((zh + 4 - s) % 4) * 2
        return Copies(lambda t, landed: (
            half_rows(chip + core, h), half_rows(chip + (1 - core if landed else core), h),
            xfs.at[s * 2 + h], xfr.at[s * 2 + h], mate))

    def step_by(axis, ty, tx, t):
        return (ty, (tx + t) % 4) if axis == "x" else ((ty + t) % 4, tx)

    def in_plane(place):
        return (zl * PLANE + place[0] * 4 + place[1], ctx)

    class Spread:
        def __init__(self, src, dst, axis, base):
            self.src, self.dst, self.axis, self.base = src, dst, axis, base
            self.cross = "y" if axis == "x" else "x"
            self.first, self.rest = [], []

        def own(self):
            for axis in (self.axis, self.cross):
                for t in (1, 3, 2):
                    at = self.base + (axis == self.cross) * 3 + t - 1

                    def make(_, landed, axis=axis, t=t, at=at):
                        py, px = step_by(axis, y, x, 4 - t) if landed else (y, x)
                        return (self.src, self.dst(py, px), wps.at[at], wpr.at[at],
                                in_plane(step_by(axis, y, x, t)))

                    (self.first if axis == self.axis else self.rest).append(Copies(make).start())

        def hand_on(self):
            for n, t in enumerate((1, 3, 2)):
                self.first[n].wait()
                for u in (1, 3, 2):
                    at = self.base + 6 + (t - 1) * 3 + u - 1

                    def make(_, landed, t=t, u=u, at=at):
                        py, px = step_by(self.axis, y, x, 4 - t)
                        ty, tx = step_by(self.cross, py, px, 4 - u) if landed else (py, px)
                        return (self.dst(py, px), self.dst(ty, tx), wps.at[at], wpr.at[at],
                                in_plane(step_by(self.cross, y, x, u)))

                    self.rest.append(Copies(make).start())

        def wait(self):
            for c in self.rest:
                c.wait()

    def from_ctx(t):
        return (ctx + 8 - t) % 8

    def all_to_all(src, dst, ss, rs):
        return Copies(lambda t, landed: (
            src.at[ctx_peer(t)], dst.at[from_ctx(t) if landed else ctx], ss.at[t], rs.at[t],
            (dp, ctx_peer(t))), 1, 8)

    mine_b = zl == core
    xb = Copies(lambda t, landed: (wbo, wb, was.at[1], war.at[1], other), where=lambda t, landed: (
        jnp.logical_not(mine_b) if landed else mine_b)).start()
    xa = across(wa, 0).start()
    to_mate_rows = [[None, None] for _ in range(4)]
    for h in range(2):
        to_mate_rows[0][h] = mate_rows(0, h).start()
    up0, down1 = own_rows(1, 0).start(), own_rows(3, 1).start()
    up1, down0 = own_rows(1, 1).start(), own_rows(3, 0).start()
    @pl.when(mine_b)
    def _():
        wb[...] = wbo[...]

    xb.wait()
    lo, hi = pl.ds(0, 512), pl.ds(512, 512)
    out_spread = [
        Spread(wb.at[:, lo], lambda py, px: wrb.at[core, py, px, :, lo], "x", 0),
        Spread(wb.at[:, hi], lambda py, px: wrb.at[core, py, px, :, hi], "y", 16),
    ]
    for w in out_spread:
        w.own()
    load_ct.wait()
    ct_mate = Copies(lambda t, landed: (
        ctc.at[core], ctc.at[1 - core if landed else core], wds.at[0], wdr.at[0], mate)).start()
    xa.wait()
    low, high = pl.ds(0, 256), pl.ds(256, 256)
    in_spread = [
        Spread(wa.at[:, :, low], lambda py, px: wra.at[:, py, px, :, low], "x", 32),
        Spread(wa.at[:, :, high], lambda py, px: wra.at[:, py, px, :, high], "y", 48),
    ]
    for w in in_spread:
        w.own()
    wrb[core, y, x] = wb[...]
    wra[:, y, x] = wa[...]
    for w in out_spread:
        w.hand_on()

    up0.wait()
    far0 = relayed_rows(1, 0).start()
    to_mate_rows[1][0] = mate_rows(1, 0).start()
    down1.wait()
    far1 = relayed_rows(3, 1).start()
    to_mate_rows[3][1] = mate_rows(3, 1).start()
    for w in in_spread:
        w.hand_on()
    up1.wait()
    to_mate_rows[1][1] = mate_rows(1, 1).start()
    down0.wait()
    to_mate_rows[3][0] = mate_rows(3, 0).start()

    for w in out_spread:
        w.wait()
    ct_mate.wait()
    ct_chip = ctc[...].reshape(BLK, D)
    wout_half = wrb[core].reshape(512, D)
    for n in range(4):
        dgs[n] = nt(wout_half[n * HD:(n + 1) * HD], ct_chip).astype(BF16)

    def head_at(n):
        return core * 4 + n

    from_half = zh // 2
    dg_sent = Copies(
        lambda t, landed: (
            dgs.at[t], dgr.at[t if landed else zh], dss.at[t], dsr.at[t if landed else zh], (dp, head_at(t))),
        0, 4,
        where=lambda t, landed: (t * 2 + from_half != ctx) if landed else (head_at(t) != ctx),
    ).start()

    @pl.when(from_half == core)
    def _():
        dgr[zh] = dgs[ctx % 4]

    for w in in_spread:
        w.wait()
    for part in range(4):
        piece = wra[:, :, :, :, part * HD:(part + 1) * HD].reshape(D, HD)
        wct[part * HD:(part + 1) * HD, :] = piece.T

    def project(zb):
        rows = xg[pl.ds(zb * 2, 2)].reshape(BLK, D)
        pre = nt(wct[...], rows)
        pret[zb] = pre
        acts = (pre * sigmoid(pre)).astype(BF16)
        actt[zb] = acts
        vrow[zb] = acts[HD:2 * HD].T
        krow[zb] = acts[3 * HD:].T

    for s in (0, 1, 3):
        for h in range(2):
            to_mate_rows[s][h].wait()
        project((zh + 4 - s) % 4)
    far0.wait()
    to_mate_rows[2][0] = mate_rows(2, 0).start()
    far1.wait()
    to_mate_rows[2][1] = mate_rows(2, 1).start()
    for h in range(2):
        to_mate_rows[2][h].wait()
    project((zh + 2) % 4)

    l0, l1, l2 = lengths_ref[0, 0], lengths_ref[0, 1], lengths_ref[0, 2]
    e0, e1, e2 = l0, l0 + l1, l0 + l1 + l2

    def forward(i):
        qpos = i * BLK + lax.broadcasted_iota(jnp.int32, (1, BLK), 1)
        first = jnp.where(qpos >= e2, e2, jnp.where(qpos >= e1, e1, jnp.where(qpos >= e0, e0, 0)))
        att = jnp.zeros((HD, BLK), F32)
        for j in range(i + 1):
            p = i * (i + 1) // 2 + j
            scores = nn(krow[j], actt[i, 2 * HD:3 * HD, :]) * SCALE + toep[i - j]
            kpos = j * BLK + lax.broadcasted_iota(jnp.int32, (BLK, BLK), 0)
            allowed = kpos >= first
            if i == j:
                allowed = allowed & (kpos <= qpos)
            sig = sigmoid(scores)
            act = scores * sig
            weights = jnp.where(allowed, act * (1.0 / SEQ), 0.0).astype(BF16)
            wts[p] = weights
            sgs[p] = jnp.where(allowed, (sig + act * (1.0 - sig)) * (1.0 / SEQ), 0.0)
            att = att + nn(actt[j, HD:2 * HD, :], weights)
        attt[i] = att

    def packed(ref, pieces):
        for n in range(2):
            rows = []
            for b in (2 * n, 2 * n + 1):
                rows += [q[:, :ROWS] for q in pieces[b]] + [q[:, ROWS:] for q in pieces[b]]
            ref[n] = jnp.concatenate(rows, axis=0)

    def unpacked(ref, r, b):
        q = ref[r, b // 2, (b % 2) * 4:(b % 2) * 4 + 4]
        return (
            jnp.concatenate([q[0:1], q[2:3]], axis=1), jnp.concatenate([q[1:2], q[3:4]], axis=1)
        )

    def to_group(src, dst, base):
        return Copies(lambda t, landed: (
            src, dst.at[from_ctx(t) if landed else ctx], sts.at[base + t], strr.at[base + t],
            (dp, ctx_peer(t))), 1, 8).start()

    for b in (3, 2, 1, 0):
        forward(b)
    pieces = []
    for b in range(NBLK):
        att = attt[b]
        mean = jnp.sum(att, axis=0, keepdims=True) * (1.0 / HD)
        cen = att - mean
        pieces.append((mean, jnp.sum(cen * cen, axis=0, keepdims=True)))
    packed(stat, pieces)
    att_stats = to_group(stat, statr, 0)
    statr[ctx] = stat[...]

    dg_sent.wait()
    grads = []
    for b in range(NBLK):
        cen = attt[b] - pieces[b][0]
        up = dgr[b].astype(F32) * actt[b, 0:HD, :].astype(F32)
        grads.append((jnp.sum(up, axis=0, keepdims=True), jnp.sum(up * cen, axis=0, keepdims=True)))
    packed(gstat, grads)
    grad_stats = to_group(gstat, gstatr, 8)
    gstatr[ctx] = gstat[...]

    att_stats.wait()
    for b in range(NBLK):
        heads = [unpacked(statr, r, b) for r in range(HEADS)]
        mean = sum([m for m, _ in heads]) * (1.0 / HEADS)
        var = 0.0
        for m, v in heads:
            var = var + v + HD * (m - mean) * (m - mean)
        inv = lax.rsqrt(var * (1.0 / D) + EPSILON)
        norm = (attt[b] - mean) * inv
        attt[b] = norm
        moments[b, 0:1] = mean
        moments[b, 1:2] = inv
        gated = (norm * actt[b, 0:HD, :].astype(F32)).astype(BF16)
        gts[2 * b] = gated[:, 0:ROWS]
        gts[2 * b + 1] = gated[:, ROWS:]
    gated_sent = all_to_all(gts, gtr, gss, gsr).start()
    gtr[ctx] = gts[ctx]
    mates_half = Copies(lambda t, landed: (
        wrb.at[core], wrb.at[1 - core if landed else core], wos.at[0], wor.at[0], mate)).start()


    def combined(b):
        mean, inv = moments[b, 0:1], moments[b, 1:2]
        s3, s4 = 0.0, 0.0
        for r in range(HEADS):
            p, q = unpacked(gstatr, r, b)
            s3 = s3 + p
            s4 = s4 + q + (unpacked(statr, r, b)[0] - mean) * p
        m1 = s3 * (1.0 / D)
        m2 = s4 * inv * (1.0 / D)
        norm = attt[b]
        dg = dgr[b].astype(F32)
        u = actt[b, 0:HD, :].astype(F32)
        dat[b] = ((dg * u - m1 - norm * m2) * inv).astype(BF16)
        uf[b] = dg * norm

    def backward(i):
        da = dat[i]
        dq = jnp.zeros((HD, BLK), F32)
        for j in range(i + 1):
            p = i * (i + 1) // 2 + j
            ds = (nn(vrow[j], da) * sgs[p]).astype(BF16)
            dq = dq + nn(actt[j, 3 * HD:, :], ds)
            dk = nt(actt[i, 2 * HD:3 * HD, :], ds)
            dv = nt(da, wts[p])
            if i < NBLK - 1:
                dk, dv = dk + dkt[j], dv + dvt[j]
            dkt[j] = dk
            dvt[j] = dv
        for part, val in enumerate((uf[i], dvt[i], dq * SCALE, dkt[i] * SCALE)):
            pre = pret[i, part * HD:(part + 1) * HD, :]
            sig = sigmoid(pre)
            dpt[i, part * HD:(part + 1) * HD, :] = (
                val * (sig * (1.0 + pre * (1.0 - sig)))
            ).astype(BF16)

    mates = {}

    def terms(b):
        theirs = pl.multiple_of((1 - core) * ROWS, ROWS)
        pd[b] = tn(dpt[b, :, pl.ds(theirs, ROWS)], wct[...]).astype(BF16)
        mates[b] = Copies(lambda t, landed: (pd.at[b], pdr.at[b], pds.at[b], pdsr.at[b], mate)).start()
        mine = pl.multiple_of(core * ROWS, ROWS)
        pm[b] = tn(dpt[b, :, pl.ds(mine, ROWS)], wct[...])

    half = (pl.ds(0, 64), pl.ds(64, 64))
    up = (dp, ((zh + 1) % 4) * 2 + core)
    down = (dp, ((zh + 3) % 4) * 2 + core)

    def round_copy(n, src, dst, to):
        return Copies(lambda t, landed: (src, dst, pss.at[n], psr.at[n], to))

    far = [
        round_copy(0, ps.at[2, half[0]], rr.at[0], up),
        round_copy(1, ps.at[2, half[1]], rr.at[1], down),
    ]
    near = {
        (1, 0): round_copy(2, ps.at[1, half[0]], pr.at[1, half[0]], up),
        (1, 1): round_copy(3, ps.at[1, half[1]], pr.at[1, half[1]], up),
        (3, 0): round_copy(4, ps.at[3, half[0]], pr.at[3, half[0]], down),
        (3, 1): round_copy(5, ps.at[3, half[1]], pr.at[3, half[1]], down),
    }
    started.extend(far)
    started.extend(near.values())

    def chip_sum(b):
        mates[b].wait()
        s = (b + 4 - zh) % 4

        @pl.when(s == 0)
        def _():
            own[...] = pm[b] + pdr[b].astype(F32)

        @pl.when(s == 2)
        def _():
            ps[2] = (pm[b] + pdr[b].astype(F32)).astype(BF16)
            far[0].go()
            far[1].go()

        @pl.when(s == 1)
        def _():
            ps[1, half[1]] = (pm[b, half[1]] + pdr[b, half[1]].astype(F32)).astype(BF16)
            near[1, 1].go()

        @pl.when(s == 3)
        def _():
            ps[3, half[0]] = (pm[b, half[0]] + pdr[b, half[0]].astype(F32)).astype(BF16)
            near[3, 0].go()

    def relay(b):
        s = (b + 4 - zh) % 4
        for n, way, h in ((0, 1, 0), (1, 3, 1)):
            @pl.when(s == way)
            def _():
                far[n].wait()
                ps[way, half[h]] = (
                    pm[b, half[h]] + pdr[b, half[h]].astype(F32) + rr[n].astype(F32)
                ).astype(BF16)
                near[way, h].go()

    def ct_cols(which):
        return jnp.concatenate(
            [ctc[which, :, pl.ds(pl.multiple_of(b * BLK + core * HD, HD), HD)] for b in range(NBLK)], axis=1
        )

    grad_stats.wait()
    combined(3)
    backward(3)
    terms(3)
    combined(2)
    backward(2)
    chip_sum(3)
    terms(2)

    combined(1)
    backward(1)
    chip_sum(2)
    terms(1)
    gated_sent.wait()
    gated_mate = Copies(lambda t, landed: (gtr, gtm, wds.at[1], wdr.at[1], mate)).start()
    combined(0)
    backward(0)
    chip_sum(1)
    terms(0)
    gated_mate.wait()
    both = jnp.concatenate([gtr[...].reshape(D, ROWS), gtm[...].reshape(D, ROWS)], axis=1)
    cts = jnp.concatenate([ct_cols(core), ct_cols(1 - core)], axis=0)
    wgs[...] = nn(both, cts).astype(BF16).reshape(2, PLANE, 32, 512)
    wg_plane = Copies(lambda t, landed: (
        wgs.at[:, plane_peer(t)], wgr.at[plane_from(t) if landed else yx], wgss.at[t], wgsr.at[t],
        (zl * PLANE + plane_peer(t), ctx)), 1, PLANE).start()
    wgr[yx] = wgs[:, yx]
    chip_sum(0)
    for b in (3, 2, 1, 0):
        relay(b)
    mates_half.wait()
    gated = gtr[...].reshape(D, ROWS)
    out_ref[...] = (
        xv[...].astype(F32)
        + tn(gated[0:512], wrb[0].reshape(512, D)) + tn(gated[512:], wrb[1].reshape(512, D))
    ).astype(BF16)

    settle([*far, *near.values(), wg_plane])
    wg_plane.wait()

    def add_plane(t, total):
        return total + wgr[t].astype(F32)

    wsum = lax.fori_loop(0, PLANE, add_plane, jnp.zeros((2, 32, 512), F32)).astype(BF16)
    for l in range(2):
        for h in range(4):
            wzs[l * 4 + h] = wsum[l, :, h * HD:(h + 1) * HD]

    zat = zl * 4 + zh

    def column(t, landed):
        to = (zat + t) % 8
        return (
            wzs.at[to], wzr.at[(zat + 8 - t) % 8 if landed else zat], wzss.at[t], wzsr.at[t],
            ((to // 4) * PLANE + yx, (to % 4) * 2 + core),
        )

    wg_column = Copies(column, 1, 8).start()
    wzr[zat] = wzs[zat]

    settle([*near.values(), wg_column])

    for c in near.values():
        c.wait()
    total = own[...] + pr[1].astype(F32) + pr[3].astype(F32)
    normed, inverse = normalize(xv[...].astype(F32))
    first = jnp.mean(total, axis=-1, keepdims=True)
    second = jnp.mean(total * normed, axis=-1, keepdims=True)
    grads_ref[...] = (
        ctc[core].astype(F32) + (total - first - normed * second) * inverse
    ).astype(BF16)

    settle([wg_column])
    wg_column.wait()
    wg_ref[...] = jnp.sum(wzr[...].astype(F32), axis=0)

    finish()


def on_device(inputs, input_weight, output_weight, cotangent, lengths, buckets, bias_weights):
    vm = lambda *shape, dt=BF16: pltpu.VMEM(shape, dt)
    sem = lambda n: pltpu.SemaphoreType.DMA((n,))
    scratch = [
        vm(8, ROWS, D), vm(2, 32, 512), vm(32, D), vm(32, D),
        vm(2, 4, 4, 32, 512), vm(2, 4, 4, 32, D),
        vm(512, D), vm(NBLK, 512, BLK, dt=F32), vm(NBLK, 512, BLK),
        vm(NBLK, BLK, HD), vm(NBLK, BLK, HD),
        vm(PAIRS, BLK, BLK), vm(PAIRS, BLK, BLK, dt=F32), vm(NBLK, BLK, BLK, dt=F32),
        vm(NBLK, HD, BLK, dt=F32), vm(NBLK, HD, BLK, dt=F32),
        vm(4, HD, BLK), vm(4, HD, BLK),
        vm(2, 8, HD, dt=F32), vm(8, 2, 8, HD, dt=F32), vm(2, 8, HD, dt=F32), vm(8, 2, 8, HD, dt=F32),
        vm(NBLK, 8, BLK, dt=F32),
        vm(8, HD, ROWS), vm(8, HD, ROWS), vm(8, HD, ROWS), vm(2, ROWS, D), vm(ROWS, D), vm(NBLK, HD, BLK),
        vm(NBLK, HD, BLK, dt=F32), vm(NBLK, HD, BLK, dt=F32),
        vm(NBLK, 512, BLK),
        vm(2, PLANE, 32, 512), vm(PLANE, 2, 32, 512),
        vm(8, 32, HD), vm(8, 32, HD),
        vm(NBLK, ROWS, D), vm(NBLK, ROWS, D), vm(NBLK, ROWS, D, dt=F32),
        vm(4, ROWS, D), vm(4, ROWS, D), vm(2, 64, D), vm(ROWS, D, dt=F32),
        sem(8), sem(8), sem(8), sem(8), sem(2), sem(2), sem(64), sem(64), sem(1), sem(1),
        sem(8), sem(8), sem(32), sem(32), sem(8), sem(8),
        sem(2), sem(2), sem(16), sem(16), sem(8), sem(8), sem(4), sem(4), sem(6), sem(6),
        sem(7),
    ]
    vspec = pl.BlockSpec(memory_space=pltpu.VMEM)
    aspec = pl.BlockSpec(memory_space=pl.ANY)
    sspec = pl.BlockSpec(memory_space=pltpu.SMEM)
    return pl.pallas_call(
        kernel,
        name="hstu",
        out_shape=(
            jax.ShapeDtypeStruct((ROWS, D), BF16),
            jax.ShapeDtypeStruct((ROWS, D), BF16),
            jax.ShapeDtypeStruct((32, HD), F32),
        ),
        in_specs=[sspec, sspec, vspec, aspec, aspec, aspec, aspec],
        out_specs=(vspec, vspec, vspec),
        scratch_shapes=scratch,
        compiler_params=pltpu.CompilerParams(
            collective_id=0, has_side_effects=True, vmem_limit_bytes=56 << 20
        ),
    )(lengths, bias_weights, buckets.reshape(1, SEQ), inputs, input_weight, output_weight, cotangent)


def solution(mesh):
    return jax.shard_map(
        on_device,
        mesh=mesh,
        in_specs=(
            P(("dp", "ctx"), None),
            P("dp", None),
            P("dp", None),
            P(("dp", "ctx"), None),
            P("dp", None),
            P(),
            P(),
        ),
        out_specs=(P(("dp", "ctx"), None), P(("dp", "ctx"), None), P("dp", "ctx")),
        check_vma=False,
    )
```

```python
import functools
import math

import jax
import jax.numpy as jnp
from jax import lax
from jax.experimental import pallas as pl
from jax.experimental.pallas import tpu as pltpu
from jax.sharding import PartitionSpec as P

EPSILON = 1e-06
MESH = pl.DeviceIdType.MESH
F32 = jnp.float32
BF16 = jnp.bfloat16

ROWS = 128
BLK = 256
NBLK = 4
HEADS = 8
HD = 128
D = 1024
SEQ = 1024
PLANE = 16
PAIRS = NBLK * (NBLK + 1) // 2
SCALE = 1.0 / math.sqrt(HD)


def nn(a, b):
    return lax.dot_general(a, b, (((1,), (0,)), ((), ())), preferred_element_type=F32)


def nt(a, b):
    return lax.dot_general(a, b, (((1,), (1,)), ((), ())), preferred_element_type=F32)


def tn(a, b):
    return lax.dot_general(a, b, (((0,), (0,)), ((), ())), preferred_element_type=F32)


def sigmoid(values):
    return 0.5 * jnp.tanh(0.5 * values) + 0.5


def normalize(values):
    average = jnp.mean(values, axis=-1, keepdims=True)
    centered = values - average
    inverse = lax.rsqrt(jnp.mean(centered * centered, axis=-1, keepdims=True) + EPSILON)
    return (centered * inverse, inverse)


def kernel(
    lengths_ref, bias_ref, buckets_ref, x_ref, win_ref, wout_ref, ct_ref,
    out_ref, grads_ref, wg_ref,
    xg, wa, wb, wbo, wra, wrb, wct, pret, actt, krow, vrow, wts, sgs, toep, attt, uf,
    dgs, dgr, stat, statr, gstat, gstatr, moments, gts, gtr, gtm, ctc, xv, dat, dkt, dvt, dpt,
    wgs, wgr, wzs, wzr,
    pd, pdr, pm, ps, pr, rr, own,
    xs, xr, xfs, xfr, was, war, wps, wpr, wos, wor, dss, dsr, sts, strr, gss, gsr,
    wds, wdr, wgss, wgsr, wzss, wzsr, pds, pdsr, pss, psr, lds,
):
    dp = lax.axis_index("dp")
    ctx = lax.axis_index("ctx")
    zh, core = ctx // 2, ctx % 2
    zl, yx = dp // PLANE, dp % PLANE
    y, x = yx // 4, yx % 4
    mate = (dp, zh * 2 + 1 - core)

    def ctx_peer(t):
        return (ctx + t) % 8

    def plane_peer(t):
        return ((y + t // 4) % 4) * 4 + (x + t % 4) % 4

    def plane_from(t):
        return ((y + 4 - t // 4) % 4) * 4 + (x + 4 - t % 4) % 4

    started = []

    class Copies:
        def __init__(self, make, lo=0, hi=1, where=None):
            self.make, self.lo, self.hi, self.where, self.received = make, lo, hi, where, False

        def each(self, act, landed=False):
            def one(t, _):
                if self.where is None:
                    run(t)
                else:
                    pl.when(self.where(t, landed))(lambda: run(t))
                return 0

            def run(t):
                src, dst, ss, rs, dev = self.make(t, landed)
                act(
                    pltpu.make_async_remote_copy(
                        src_ref=src, dst_ref=dst, send_sem=ss, recv_sem=rs,
                        device_id=dev, device_id_type=MESH,
                    )
                )

            if self.hi - self.lo == 1:
                one(self.lo, 0)
            else:
                lax.fori_loop(self.lo, self.hi, one, 0)

        def go(self):
            self.each(lambda c: c.start())

        def start(self):
            started.append(self)
            self.go()
            return self

        def wait(self):
            self.received = True
            self.each(lambda c: c.wait_recv(), True)

        def sent(self):
            self.each(lambda c: c.wait_send())

    def settle(later=()):
        for c in [c for c in started if c not in later]:
            c.sent()
            started.remove(c)

    def finish():
        for c in started:
            if not c.received:
                c.wait()
        settle()

    barrier = pltpu.get_barrier_semaphore()

    def greet_ctx(t, _):
        pl.semaphore_signal(barrier, inc=1, device_id=(dp, ctx_peer(t)), device_id_type=MESH)
        return 0

    def greet_plane(t, _):
        pl.semaphore_signal(
            barrier, inc=1, device_id=(zl * PLANE + plane_peer(t), ctx), device_id_type=MESH
        )
        return 0

    def greet_column(t, _):
        pl.semaphore_signal(
            barrier, inc=1, device_id=((1 - zl) * PLANE + yx, t * 2 + core), device_id_type=MESH
        )
        return 0

    lax.fori_loop(1, 8, greet_ctx, 0)
    lax.fori_loop(1, 16, greet_plane, 0)
    lax.fori_loop(0, 4, greet_column, 0)

    load_x = pltpu.make_async_copy(x_ref, xv, lds.at[0])
    load_x.start()
    load_w = [
        pltpu.make_async_copy(wout_ref, wbo, lds.at[1])
    ]
    for part in range(4):
        at = pl.multiple_of(part * D + ctx * HD, HD)
        load_w.append(
            pltpu.make_async_copy(
                win_ref.at[:, pl.ds(at, HD)], wa.at[zl, :, pl.ds(part * HD, HD)], lds.at[2 + part]
            )
        )
    for c in load_w:
        c.start()
    load_ct = pltpu.make_async_copy(ct_ref, ctc.at[core], lds.at[6])
    load_ct.start()
    load_x.wait()
    normed, _ = normalize(xv[...].astype(F32))
    xg[ctx] = normed.astype(BF16)
    for c in load_w:
        c.wait()

    buckets = buckets_ref[...]
    table = jnp.zeros((1, SEQ), F32)
    for b in range(32):
        table = jnp.where(buckets == b, bias_ref[ctx, b], table)
    padded = jnp.concatenate([table[:, 0:BLK], table], axis=1)
    for d in range(NBLK):
        wide = jnp.broadcast_to(padded[:, d * BLK:d * BLK + 2 * BLK], (BLK, 2 * BLK))
        toep[d] = pltpu.roll(wide, 0, 1, stride=1, stride_axis=0)[:, BLK:]

    pl.semaphore_wait(barrier, 26)

    other = ((1 - zl) * PLANE + yx, ctx)

    def across(ref, k):
        return Copies(lambda t, landed: (
            ref.at[zl], ref.at[1 - zl if landed else zl], was.at[k], war.at[k], other))

    def half_rows(r, h):
        return xg.at[r, pl.ds(h * 64, 64)]

    def own_rows(s, h):
        src = ((zh + 4 - s) % 4) * 2 + core
        return Copies(lambda t, landed: (
            half_rows(ctx, h), half_rows(src if landed else ctx, h), xs.at[s * 2 + h], xr.at[s * 2 + h],
            (dp, ((zh + s) % 4) * 2 + core)))

    def relayed_rows(s, h):
        src = ((zh + 4 - s) % 4) * 2 + core
        far = ((zh + 2) % 4) * 2 + core
        return Copies(lambda t, landed: (
            half_rows(src, h), half_rows(far if landed else src, h), xs.at[4 + h], xr.at[4 + h],
            (dp, ((zh + s) % 4) * 2 + core)))

    def mate_rows(s, h):
        chip = ((zh + 4 - s) % 4) * 2
        return Copies(lambda t, landed: (
            half_rows(chip + core, h), half_rows(chip + (1 - core if landed else core), h),
            xfs.at[s * 2 + h], xfr.at[s * 2 + h], mate))

    def step_by(axis, ty, tx, t):
        return (ty, (tx + t) % 4) if axis == "x" else ((ty + t) % 4, tx)

    def in_plane(place):
        return (zl * PLANE + place[0] * 4 + place[1], ctx)

    class Spread:
        def __init__(self, src, dst, axis, base):
            self.src, self.dst, self.axis, self.base = src, dst, axis, base
            self.cross = "y" if axis == "x" else "x"
            self.first, self.rest = [], []

        def own(self, part=None, k=0):
            src = self.src if part is None else self.src.at[part]
            for axis in (self.axis, self.cross):
                for t in (1, 3, 2):
                    at = self.base + 6 * k + (axis == self.cross) * 3 + t - 1

                    def make(_, landed, axis=axis, t=t, at=at):
                        py, px = step_by(axis, y, x, 4 - t) if landed else (y, x)
                        dst = self.dst(py, px)
                        return (src, dst if part is None else dst.at[part], wps.at[at], wpr.at[at],
                                in_plane(step_by(axis, y, x, t)))

                    (self.first if axis == self.axis else self.rest).append(Copies(make).start())

        def hand_on(self):
            for n, t in enumerate((1, 3, 2)):
                for c in self.first[n::3]:
                    c.wait()
                for u in (1, 3, 2):
                    at = self.base + 12 + (t - 1) * 3 + u - 1

                    def make(_, landed, t=t, u=u, at=at):
                        py, px = step_by(self.axis, y, x, 4 - t)
                        ty, tx = step_by(self.cross, py, px, 4 - u) if landed else (py, px)
                        return (self.dst(py, px), self.dst(ty, tx), wps.at[at], wpr.at[at],
                                in_plane(step_by(self.cross, y, x, u)))

                    self.rest.append(Copies(make).start())

        def wait(self):
            for c in self.rest:
                c.wait()

    def from_ctx(t):
        return (ctx + 8 - t) % 8

    def all_to_all(src, dst, ss, rs):
        return Copies(lambda t, landed: (
            src.at[ctx_peer(t)], dst.at[from_ctx(t) if landed else ctx], ss.at[t], rs.at[t],
            (dp, ctx_peer(t))), 1, 8)

    mine_b = zl == core
    xb = Copies(lambda t, landed: (wbo, wb, was.at[1], war.at[1], other), where=lambda t, landed: (
        jnp.logical_not(mine_b) if landed else mine_b)).start()
    xa = across(wa, 0).start()
    to_mate_rows = [[None, None] for _ in range(4)]
    for h in range(2):
        to_mate_rows[0][h] = mate_rows(0, h).start()
    up0, down1 = own_rows(1, 0).start(), own_rows(3, 1).start()
    up1, down0 = own_rows(1, 1).start(), own_rows(3, 0).start()
    @pl.when(mine_b)
    def _():
        wb[...] = wbo[...]

    low, high = pl.ds(0, 256), pl.ds(256, 256)
    in_spread = [
        Spread(wa.at[:, :, low], lambda py, px: wra.at[:, py, px, :, low], "x", 48),
        Spread(wa.at[:, :, high], lambda py, px: wra.at[:, py, px, :, high], "y", 72),
    ]
    for w in in_spread:
        w.own(pl.ds(zl, 1), 0)
    xb.wait()
    lo, hi = pl.ds(0, 512), pl.ds(512, 512)
    out_spread = [
        Spread(wb.at[:, lo], lambda py, px: wrb.at[core, py, px, :, lo], "x", 0),
        Spread(wb.at[:, hi], lambda py, px: wrb.at[core, py, px, :, hi], "y", 24),
    ]
    for w in out_spread:
        w.own()
    load_ct.wait()
    ct_mate = Copies(lambda t, landed: (
        ctc.at[core], ctc.at[1 - core if landed else core], wds.at[0], wdr.at[0], mate)).start()
    xa.wait()
    for w in in_spread:
        w.own(pl.ds(1 - zl, 1), 1)
    wrb[core, y, x] = wb[...]
    wra[:, y, x] = wa[...]
    for w in out_spread:
        w.hand_on()

    up0.wait()
    far0 = relayed_rows(1, 0).start()
    to_mate_rows[1][0] = mate_rows(1, 0).start()
    down1.wait()
    far1 = relayed_rows(3, 1).start()
    to_mate_rows[3][1] = mate_rows(3, 1).start()
    for w in in_spread:
        w.hand_on()
    up1.wait()
    to_mate_rows[1][1] = mate_rows(1, 1).start()
    down0.wait()
    to_mate_rows[3][0] = mate_rows(3, 0).start()

    for w in out_spread:
        w.wait()
    ct_mate.wait()
    ct_chip = ctc[...].reshape(BLK, D)
    wout_half = wrb[core].reshape(512, D)
    for n in range(4):
        dgs[n] = nt(wout_half[n * HD:(n + 1) * HD], ct_chip).astype(BF16)

    def head_at(n):
        return core * 4 + n

    from_half = zh // 2
    dg_sent = Copies(
        lambda t, landed: (
            dgs.at[t], dgr.at[t if landed else zh], dss.at[t], dsr.at[t if landed else zh], (dp, head_at(t))),
        0, 4,
        where=lambda t, landed: (t * 2 + from_half != ctx) if landed else (head_at(t) != ctx),
    ).start()

    @pl.when(from_half == core)
    def _():
        dgr[zh] = dgs[ctx % 4]

    for w in in_spread:
        w.wait()
    for part in range(4):
        piece = wra[:, :, :, :, part * HD:(part + 1) * HD].reshape(D, HD)
        wct[part * HD:(part + 1) * HD, :] = piece.T

    def project(zb):
        rows = xg[pl.ds(zb * 2, 2)].reshape(BLK, D)
        pre = nt(wct[...], rows)
        pret[zb] = pre
        acts = (pre * sigmoid(pre)).astype(BF16)
        actt[zb] = acts
        vrow[zb] = acts[HD:2 * HD].T
        krow[zb] = acts[3 * HD:].T

    for s in (0, 1, 3):
        for h in range(2):
            to_mate_rows[s][h].wait()
        project((zh + 4 - s) % 4)
    far0.wait()
    to_mate_rows[2][0] = mate_rows(2, 0).start()
    far1.wait()
    to_mate_rows[2][1] = mate_rows(2, 1).start()
    for h in range(2):
        to_mate_rows[2][h].wait()
    project((zh + 2) % 4)

    l0, l1, l2 = lengths_ref[0, 0], lengths_ref[0, 1], lengths_ref[0, 2]
    e0, e1, e2 = l0, l0 + l1, l0 + l1 + l2

    def forward(i):
        qpos = i * BLK + lax.broadcasted_iota(jnp.int32, (1, BLK), 1)
        first = jnp.where(qpos >= e2, e2, jnp.where(qpos >= e1, e1, jnp.where(qpos >= e0, e0, 0)))
        att = jnp.zeros((HD, BLK), F32)
        for j in range(i + 1):
            p = i * (i + 1) // 2 + j
            scores = nn(krow[j], actt[i, 2 * HD:3 * HD, :]) * SCALE + toep[i - j]
            kpos = j * BLK + lax.broadcasted_iota(jnp.int32, (BLK, BLK), 0)
            allowed = kpos >= first
            if i == j:
                allowed = allowed & (kpos <= qpos)
            sig = sigmoid(scores)
            act = scores * sig
            weights = jnp.where(allowed, act * (1.0 / SEQ), 0.0).astype(BF16)
            wts[p] = weights
            sgs[p] = jnp.where(allowed, (sig + act * (1.0 - sig)) * (1.0 / SEQ), 0.0)
            att = att + nn(actt[j, HD:2 * HD, :], weights)
        attt[i] = att

    def packed(ref, pieces):
        for n in range(2):
            rows = []
            for b in (2 * n, 2 * n + 1):
                rows += [q[:, :ROWS] for q in pieces[b]] + [q[:, ROWS:] for q in pieces[b]]
            ref[n] = jnp.concatenate(rows, axis=0)

    def unpacked(ref, r, b):
        q = ref[r, b // 2, (b % 2) * 4:(b % 2) * 4 + 4]
        return (
            jnp.concatenate([q[0:1], q[2:3]], axis=1), jnp.concatenate([q[1:2], q[3:4]], axis=1)
        )

    def to_group(src, dst, base):
        return Copies(lambda t, landed: (
            src, dst.at[from_ctx(t) if landed else ctx], sts.at[base + t], strr.at[base + t],
            (dp, ctx_peer(t))), 1, 8).start()

    for b in (3, 2, 1, 0):
        forward(b)
    pieces = []
    for b in range(NBLK):
        att = attt[b]
        mean = jnp.sum(att, axis=0, keepdims=True) * (1.0 / HD)
        cen = att - mean
        pieces.append((mean, jnp.sum(cen * cen, axis=0, keepdims=True)))
    packed(stat, pieces)
    att_stats = to_group(stat, statr, 0)
    statr[ctx] = stat[...]

    dg_sent.wait()
    grads = []
    for b in range(NBLK):
        cen = attt[b] - pieces[b][0]
        up = dgr[b].astype(F32) * actt[b, 0:HD, :].astype(F32)
        grads.append((jnp.sum(up, axis=0, keepdims=True), jnp.sum(up * cen, axis=0, keepdims=True)))
    packed(gstat, grads)
    grad_stats = to_group(gstat, gstatr, 8)
    gstatr[ctx] = gstat[...]

    att_stats.wait()
    for b in range(NBLK):
        heads = [unpacked(statr, r, b) for r in range(HEADS)]
        mean = sum([m for m, _ in heads]) * (1.0 / HEADS)
        var = 0.0
        for m, v in heads:
            var = var + v + HD * (m - mean) * (m - mean)
        inv = lax.rsqrt(var * (1.0 / D) + EPSILON)
        norm = (attt[b] - mean) * inv
        attt[b] = norm
        moments[b, 0:1] = mean
        moments[b, 1:2] = inv
        gated = (norm * actt[b, 0:HD, :].astype(F32)).astype(BF16)
        gts[2 * b] = gated[:, 0:ROWS]
        gts[2 * b + 1] = gated[:, ROWS:]
    gated_sent = all_to_all(gts, gtr, gss, gsr).start()
    gtr[ctx] = gts[ctx]
    mates_half = Copies(lambda t, landed: (
        wrb.at[core], wrb.at[1 - core if landed else core], wos.at[0], wor.at[0], mate)).start()


    def combined(b):
        mean, inv = moments[b, 0:1], moments[b, 1:2]
        s3, s4 = 0.0, 0.0
        for r in range(HEADS):
            p, q = unpacked(gstatr, r, b)
            s3 = s3 + p
            s4 = s4 + q + (unpacked(statr, r, b)[0] - mean) * p
        m1 = s3 * (1.0 / D)
        m2 = s4 * inv * (1.0 / D)
        norm = attt[b]
        dg = dgr[b].astype(F32)
        u = actt[b, 0:HD, :].astype(F32)
        dat[b] = ((dg * u - m1 - norm * m2) * inv).astype(BF16)
        uf[b] = dg * norm

    def backward(i):
        da = dat[i]
        dq = jnp.zeros((HD, BLK), F32)
        for j in range(i + 1):
            p = i * (i + 1) // 2 + j
            ds = (nn(vrow[j], da) * sgs[p]).astype(BF16)
            dq = dq + nn(actt[j, 3 * HD:, :], ds)
            dk = nt(actt[i, 2 * HD:3 * HD, :], ds)
            dv = nt(da, wts[p])
            if i < NBLK - 1:
                dk, dv = dk + dkt[j], dv + dvt[j]
            dkt[j] = dk
            dvt[j] = dv
        for part, val in enumerate((uf[i], dvt[i], dq * SCALE, dkt[i] * SCALE)):
            pre = pret[i, part * HD:(part + 1) * HD, :]
            sig = sigmoid(pre)
            dpt[i, part * HD:(part + 1) * HD, :] = (
                val * (sig * (1.0 + pre * (1.0 - sig)))
            ).astype(BF16)

    mates = {}

    def terms(b):
        theirs = pl.multiple_of((1 - core) * ROWS, ROWS)
        pd[b] = tn(dpt[b, :, pl.ds(theirs, ROWS)], wct[...]).astype(BF16)
        mates[b] = Copies(lambda t, landed: (pd.at[b], pdr.at[b], pds.at[b], pdsr.at[b], mate)).start()
        mine = pl.multiple_of(core * ROWS, ROWS)
        pm[b] = tn(dpt[b, :, pl.ds(mine, ROWS)], wct[...])

    half = (pl.ds(0, 64), pl.ds(64, 64))
    up = (dp, ((zh + 1) % 4) * 2 + core)
    down = (dp, ((zh + 3) % 4) * 2 + core)

    def round_copy(n, src, dst, to):
        return Copies(lambda t, landed: (src, dst, pss.at[n], psr.at[n], to))

    far = [
        round_copy(0, ps.at[2, half[0]], rr.at[0], up),
        round_copy(1, ps.at[2, half[1]], rr.at[1], down),
    ]
    near = {
        (1, 0): round_copy(2, ps.at[1, half[0]], pr.at[1, half[0]], up),
        (1, 1): round_copy(3, ps.at[1, half[1]], pr.at[1, half[1]], up),
        (3, 0): round_copy(4, ps.at[3, half[0]], pr.at[3, half[0]], down),
        (3, 1): round_copy(5, ps.at[3, half[1]], pr.at[3, half[1]], down),
    }
    started.extend(far)
    started.extend(near.values())

    def chip_sum(b):
        mates[b].wait()
        s = (b + 4 - zh) % 4

        @pl.when(s == 0)
        def _():
            own[...] = pm[b] + pdr[b].astype(F32)

        @pl.when(s == 2)
        def _():
            ps[2] = (pm[b] + pdr[b].astype(F32)).astype(BF16)
            far[0].go()
            far[1].go()

        @pl.when(s == 1)
        def _():
            ps[1, half[1]] = (pm[b, half[1]] + pdr[b, half[1]].astype(F32)).astype(BF16)
            near[1, 1].go()

        @pl.when(s == 3)
        def _():
            ps[3, half[0]] = (pm[b, half[0]] + pdr[b, half[0]].astype(F32)).astype(BF16)
            near[3, 0].go()

    def relay(b):
        s = (b + 4 - zh) % 4
        for n, way, h in ((0, 1, 0), (1, 3, 1)):
            @pl.when(s == way)
            def _():
                far[n].wait()
                ps[way, half[h]] = (
                    pm[b, half[h]] + pdr[b, half[h]].astype(F32) + rr[n].astype(F32)
                ).astype(BF16)
                near[way, h].go()

    def ct_cols(which):
        return jnp.concatenate(
            [ctc[which, :, pl.ds(pl.multiple_of(b * BLK + core * HD, HD), HD)] for b in range(NBLK)], axis=1
        )

    grad_stats.wait()
    combined(3)
    backward(3)
    terms(3)
    combined(2)
    backward(2)
    chip_sum(3)
    terms(2)

    combined(1)
    backward(1)
    chip_sum(2)
    gated_sent.wait()
    gated_mate = Copies(lambda t, landed: (gtr, gtm, wds.at[1], wdr.at[1], mate)).start()
    terms(1)
    combined(0)
    backward(0)
    chip_sum(1)
    gated_mate.wait()
    both = jnp.concatenate([gtr[...].reshape(D, ROWS), gtm[...].reshape(D, ROWS)], axis=1)
    cts = jnp.concatenate([ct_cols(core), ct_cols(1 - core)], axis=0)
    wgs[...] = nn(both, cts).astype(BF16).reshape(2, PLANE, 32, 512)
    wg_plane = Copies(lambda t, landed: (
        wgs.at[:, plane_peer(t)], wgr.at[plane_from(t) if landed else yx], wgss.at[t], wgsr.at[t],
        (zl * PLANE + plane_peer(t), ctx)), 1, PLANE).start()
    wgr[yx] = wgs[:, yx]
    terms(0)
    chip_sum(0)
    for b in (3, 2, 1, 0):
        relay(b)
    mates_half.wait()
    gated = gtr[...].reshape(D, ROWS)
    out_ref[...] = (
        xv[...].astype(F32)
        + tn(gated[0:512], wrb[0].reshape(512, D)) + tn(gated[512:], wrb[1].reshape(512, D))
    ).astype(BF16)

    settle([*far, *near.values(), wg_plane])
    wg_plane.wait()

    def add_plane(t, total):
        return total + wgr[t].astype(F32)

    wsum = lax.fori_loop(0, PLANE, add_plane, jnp.zeros((2, 32, 512), F32)).astype(BF16)
    for l in range(2):
        for h in range(4):
            wzs[l * 4 + h] = wsum[l, :, h * HD:(h + 1) * HD]

    zat = zl * 4 + zh

    def column(t, landed):
        to = (zat + t) % 8
        return (
            wzs.at[to], wzr.at[(zat + 8 - t) % 8 if landed else zat], wzss.at[t], wzsr.at[t],
            ((to // 4) * PLANE + yx, (to % 4) * 2 + core),
        )

    wg_column = Copies(column, 1, 8).start()
    wzr[zat] = wzs[zat]

    settle([*near.values(), wg_column])

    for c in near.values():
        c.wait()
    total = own[...] + pr[1].astype(F32) + pr[3].astype(F32)
    normed, inverse = normalize(xv[...].astype(F32))
    first = jnp.mean(total, axis=-1, keepdims=True)
    second = jnp.mean(total * normed, axis=-1, keepdims=True)
    grads_ref[...] = (
        ctc[core].astype(F32) + (total - first - normed * second) * inverse
    ).astype(BF16)

    settle([wg_column])
    wg_column.wait()
    wg_ref[...] = jnp.sum(wzr[...].astype(F32), axis=0)

    finish()


def on_device(inputs, input_weight, output_weight, cotangent, lengths, buckets, bias_weights):
    vm = lambda *shape, dt=BF16: pltpu.VMEM(shape, dt)
    sem = lambda n: pltpu.SemaphoreType.DMA((n,))
    scratch = [
        vm(8, ROWS, D), vm(2, 32, 512), vm(32, D), vm(32, D),
        vm(2, 4, 4, 32, 512), vm(2, 4, 4, 32, D),
        vm(512, D), vm(NBLK, 512, BLK, dt=F32), vm(NBLK, 512, BLK),
        vm(NBLK, BLK, HD), vm(NBLK, BLK, HD),
        vm(PAIRS, BLK, BLK), vm(PAIRS, BLK, BLK, dt=F32), vm(NBLK, BLK, BLK, dt=F32),
        vm(NBLK, HD, BLK, dt=F32), vm(NBLK, HD, BLK, dt=F32),
        vm(4, HD, BLK), vm(4, HD, BLK),
        vm(2, 8, HD, dt=F32), vm(8, 2, 8, HD, dt=F32), vm(2, 8, HD, dt=F32), vm(8, 2, 8, HD, dt=F32),
        vm(NBLK, 8, BLK, dt=F32),
        vm(8, HD, ROWS), vm(8, HD, ROWS), vm(8, HD, ROWS), vm(2, ROWS, D), vm(ROWS, D), vm(NBLK, HD, BLK),
        vm(NBLK, HD, BLK, dt=F32), vm(NBLK, HD, BLK, dt=F32),
        vm(NBLK, 512, BLK),
        vm(2, PLANE, 32, 512), vm(PLANE, 2, 32, 512),
        vm(8, 32, HD), vm(8, 32, HD),
        vm(NBLK, ROWS, D), vm(NBLK, ROWS, D), vm(NBLK, ROWS, D, dt=F32),
        vm(4, ROWS, D), vm(4, ROWS, D), vm(2, 64, D), vm(ROWS, D, dt=F32),
        sem(8), sem(8), sem(8), sem(8), sem(2), sem(2), sem(96), sem(96), sem(1), sem(1),
        sem(8), sem(8), sem(32), sem(32), sem(8), sem(8),
        sem(2), sem(2), sem(16), sem(16), sem(8), sem(8), sem(4), sem(4), sem(6), sem(6),
        sem(7),
    ]
    vspec = pl.BlockSpec(memory_space=pltpu.VMEM)
    aspec = pl.BlockSpec(memory_space=pl.ANY)
    sspec = pl.BlockSpec(memory_space=pltpu.SMEM)
    return pl.pallas_call(
        kernel,
        name="hstu",
        out_shape=(
            jax.ShapeDtypeStruct((ROWS, D), BF16),
            jax.ShapeDtypeStruct((ROWS, D), BF16),
            jax.ShapeDtypeStruct((32, HD), F32),
        ),
        in_specs=[sspec, sspec, vspec, aspec, aspec, aspec, aspec],
        out_specs=(vspec, vspec, vspec),
        scratch_shapes=scratch,
        compiler_params=pltpu.CompilerParams(
            collective_id=0, has_side_effects=True, vmem_limit_bytes=56 << 20
        ),
    )(lengths, bias_weights, buckets.reshape(1, SEQ), inputs, input_weight, output_weight, cotangent)


def solution(mesh):
    return jax.shard_map(
        on_device,
        mesh=mesh,
        in_specs=(
            P(("dp", "ctx"), None),
            P("dp", None),
            P("dp", None),
            P(("dp", "ctx"), None),
            P("dp", None),
            P(),
            P(),
        ),
        out_specs=(P(("dp", "ctx"), None), P(("dp", "ctx"), None), P("dp", "ctx")),
        check_vma=False,
    )
```
